32 devices in a mesh: tm: 16 (over z, x, core), space: 2 (over y).
Axes of the slice: x: 2, y: 2, z: 4, core: 2. Of those that a mesh axis runs over, the one named last changes fastest.
Arguments:
- field: float32 [256, 64, 2048], P('tm', 'space'), may hold values from -3 to 3
- step: float32 [1], replicated, may hold values from 9.9e-05 to 0.001
- mass: float32 [1], replicated, may hold values from 0.02 to 0.05
Outputs:
- field_out: float32 [256, 64, 2048], P('tm', 'space')
The draws below stay inside these ranges and needn't reach their ends.
All inputs are finite; a program needn't handle non-finite values.
Results may differ from the reference program's by a relative error of at most 0.0001.
Values sent between devices are 32-bit elements; how exact they have to be, the bound alone decides.
No kernel may reach another device: no remote copies, remote signals or barrier semaphores. Data moves between devices by JAX's collectives and lax.ppermute only.
A program may use at most 64 MiB of HBM per device.

```python
import jax
import jax.numpy as jnp
from jax import lax

NT = 256
NY = 64
NZ = 32
ITERS = 2
NX = 64


def scalar_pair(key):
    mass_key = jax.random.fold_in(key, 7)
    ratio_key = jax.random.fold_in(key, 13)
    mass_value = jax.random.uniform(mass_key, (1,), jnp.float32, 0.02, 0.05)
    step_ratio = jax.random.uniform(ratio_key, (1,), jnp.float32, 0.25, 0.4)
    return (mass_value, step_ratio * mass_value * mass_value)


def draw_step(key, part):
    return scalar_pair(key)[1]


def draw_mass(key, part):
    return scalar_pair(key)[0]


def level_of(stream_key, extent, pieces, smallest, top_value):
    loudness = 1.0
    for dim, shards_of in pieces:
        steps = jax.random.uniform(jax.random.fold_in(jax.random.fold_in(stream_key, 6), dim), (shards_of,), jnp.float32, smallest / len(pieces), top_value / len(pieces))
        loudness = loudness * jnp.repeat(jnp.exp(steps), extent[dim] // shards_of).reshape((-1,) + (1,) * (len(extent) - 1 - dim))
    return loudness


def normal_values(own_key, dims, deviation, limit, pieces=(), kind=jnp.bfloat16):
    array = deviation * jax.random.normal(own_key, dims, jnp.float32)
    if pieces:
        array = array * level_of(own_key, dims, pieces, -0.22, 0.18)
    return jnp.clip(array, -limit, limit).astype(kind)


def setup_inputs(seed: int = 0) -> dict:
    key_of = jax.random.split(jax.random.key(seed), 4)
    field = normal_values(key_of[0], (NT, NX, NY * NZ), 0.7, 3.0, ((0, 16), (1, 2)), jnp.float32)
    step = draw_step(jax.random.fold_in(key_of[3], 71), 0)
    mass = draw_mass(jax.random.fold_in(key_of[3], 71), 0)
    return {"field": field, "step": step, "mass": mass}


def laplacian(field):
    total = jnp.roll(field, 1, axis=0) + jnp.roll(field, -1, axis=0) - 8.0 * field
    padded = jnp.pad(field, ((0, 0), (1, 1), (1, 1), (1, 1)))
    total = total + padded[:, 2:, 1:-1, 1:-1] + padded[:, :-2, 1:-1, 1:-1]
    total = total + padded[:, 1:-1, 2:, 1:-1] + padded[:, 1:-1, :-2, 1:-1]
    total = total + padded[:, 1:-1, 1:-1, 2:] + padded[:, 1:-1, 1:-1, :-2]
    return total


def reference(field, step, mass):
    field = field.reshape(NT, NX, NY, NZ)
    wave = jnp.arange(NT).astype(jnp.float32)
    symbol = mass[0] * mass[0] + 4.0 * jnp.sin(jnp.pi * wave / NT) ** 2
    for turn in range(ITERS):
        force = -laplacian(field) + field - 0.9 * field * field + 0.25 * field * field * field
        planes = jnp.moveaxis(force, 1, 0)

        def solve_plane(plane):
            spectrum = jnp.fft.fft(plane, axis=0) / symbol[:, None, None]
            return jnp.real(jnp.fft.ifft(spectrum, axis=0)).astype(field.dtype)

        update = jnp.moveaxis(lax.map(solve_plane, planes), 0, 1)
        field = field - step[0] * update
    return field.reshape(NT, NX, NY * NZ)
```

```python
import jax
import jax.numpy as jnp
from jax import lax
from jax.experimental import pallas as pl
from jax.experimental.pallas import tpu as pltpu
from jax.sharding import PartitionSpec as P

NZ = 32
ITERS = 2

LANES = 128
ROWS = 8


def decay(mass):
    root = jnp.sqrt(1.0 + 0.25 * mass * mass)
    return 1.0 + 0.5 * mass * mass - mass * root, 0.5 / (mass * root)


def relax(phi, step_ref, mass_ref, psi_ref, ends_ref, tiles):
    slices, planes, _ = psi_ref.shape
    blocks = planes // ROWS
    lane = lax.broadcasted_iota(jnp.int32, (ROWS, LANES), 1)
    row = lax.broadcasted_iota(jnp.int32, (ROWS, LANES), 0)
    mass = jnp.full((ROWS, LANES), mass_ref[0], jnp.float32)
    step = jnp.full((ROWS, LANES), step_ref[0], jnp.float32)
    r, amplitude = decay(mass)
    scale = step * amplitude
    c1, c2, c3 = scale * (7.0 - mass * mass), -0.9 * scale, 0.25 * scale
    keep = 1.0 - step
    first_z, last_z = lane % NZ == 0, lane % NZ == NZ - 1
    first_row, last_row = row == 0, row == ROWS - 1
    head, tail = lane < NZ, lane >= LANES - NZ
    zero = jnp.zeros((ROWS, LANES), jnp.float32)

    def at(t, i, start):
        return phi[t, ROWS * i : ROWS * (i + 1), pl.ds(start, LANES)]

    def tile(j, carry):
        start = pl.multiple_of((j + 1) * LANES, LANES)
        out = pl.ds(pl.multiple_of(j * LANES, LANES), LANES)
        for i in range(blocks):
            force = [None] * slices
            for k in range(slices):
                t = k // 2 if k % 2 == 0 else slices - 1 - k // 2
                v = at(t, i, start)
                before = zero if i == 0 else at(t, i - 1, start)
                after = zero if i == blocks - 1 else at(t, i + 1, start)
                total = pltpu.roll(jnp.where(last_row, before, v), 1, 0)
                total = total + pltpu.roll(jnp.where(first_row, after, v), ROWS - 1, 0)
                total = total + jnp.where(first_z, 0.0, pltpu.roll(v, 1, 1))
                total = total + jnp.where(last_z, 0.0, pltpu.roll(v, LANES - 1, 1))
                total = total + pltpu.roll(jnp.where(tail, at(t, i, start - LANES), v), NZ, 1)
                total = total + pltpu.roll(jnp.where(head, at(t, i, start + LANES), v), LANES - NZ, 1)
                force[t] = v * (c1 + v * (c2 + c3 * v)) - scale * total
            forward, backward = [None] * slices, [None] * slices
            a, b = force[0], force[-1]
            forward[0], backward[-1] = None, b
            for t in range(1, slices):
                forward[t] = r * a
                a = force[t] + forward[t]
                s = slices - 1 - t
                b = force[s] + r * b
                backward[s] = b
            rows = slice(ROWS * i, ROWS * (i + 1))
            ends_ref[0, rows, out] = a
            ends_ref[1, rows, out] = b
            for t in range(slices):
                local = backward[t] if t == 0 else forward[t] + backward[t]
                psi_ref[t, rows, out] = keep * at(t, i, start) - local
        return carry

    lax.fori_loop(tiles[0], tiles[1], tile, 0)


def clear_guards(phi):
    slices, planes, width = phi.shape
    guard = jnp.zeros((slices, planes, LANES), jnp.float32)
    phi[:, :, :LANES] = guard
    phi[:, :, width - LANES :] = guard


def first_kernel(step_ref, mass_ref, field_ref, psi_ref, ends_ref, phi, sems):
    width = psi_ref.shape[-1]
    parts = sems.shape[0]
    part = width // parts
    copies = []
    for n in range(parts):
        copies.append(
            pltpu.make_async_copy(
                field_ref.at[:, :, n * part : (n + 1) * part],
                phi.at[:, :, LANES + n * part : LANES + (n + 1) * part],
                sems.at[n],
            )
        )
        copies[-1].start()
    clear_guards(phi)
    copies[0].wait()
    for n in range(parts):
        if n + 1 < parts:
            copies[n + 1].wait()
        relax(phi, step_ref, mass_ref, psi_ref, ends_ref, (n * part // LANES, (n + 1) * part // LANES))


def next_kernel(core_ref, step_ref, mass_ref, own_ref, other_ref, low_ref, high_ref, old_ref, psi_ref, ends_ref, phi):
    slices, planes, width = psi_ref.shape
    blocks = planes // ROWS
    mass = jnp.full((ROWS, LANES), mass_ref[0], jnp.float32)
    r, _ = decay(mass)
    inverse = 1.0 / r
    last = r
    for _ in range(slices - 1):
        last = last * r
    row = lax.broadcasted_iota(jnp.int32, (ROWS, LANES), 0)
    core = core_ref[0]
    clear_guards(phi)

    def tile(j, carry):
        lanes = pl.ds(pl.multiple_of(j * LANES, LANES), LANES)
        inner = pl.ds(pl.multiple_of((j + 1) * LANES, LANES), LANES)
        for i in range(blocks):
            rows = slice(ROWS * i, ROWS * (i + 1))
            half = 2 * i // blocks
            place = slice(ROWS * i - half * planes // 2, ROWS * (i + 1) - half * planes // 2)
            mine = core == half
            p = jnp.where(mine, own_ref[0, place, lanes], other_ref[0, place, lanes]) * r
            q = jnp.where(mine, own_ref[1, place, lanes], other_ref[1, place, lanes]) * last
            for t in range(slices):
                value = old_ref[t, rows, lanes] - p - q
                if i == 0:
                    value = value + jnp.where(row == 0, low_ref[t : t + 1, lanes], 0.0)
                if i == blocks - 1:
                    value = value + jnp.where(row == ROWS - 1, high_ref[t : t + 1, lanes], 0.0)
                phi[t, rows, inner] = value
                p, q = p * r, q * inverse
        return carry

    lax.fori_loop(0, width // LANES, tile, 0)
    relax(phi, step_ref, mass_ref, psi_ref, ends_ref, (0, width // LANES))


VMEM = pl.BlockSpec(memory_space=pltpu.VMEM)
SMEM = pl.BlockSpec(memory_space=pltpu.SMEM)


def outputs_of(shape):
    slices, planes, width = shape
    return dict(
        out_shape=(
            jax.ShapeDtypeStruct(shape, jnp.float32),
            jax.ShapeDtypeStruct((2, planes, width), jnp.float32),
        ),
        out_specs=(VMEM, VMEM),
        compiler_params=pltpu.CompilerParams(vmem_limit_bytes=24 * 2**20),
        cost_estimate=pl.CostEstimate(flops=30 * slices * planes * width, bytes_accessed=8 * slices * planes * width, transcendentals=0),
    )


def first_relax(field, step, mass):
    slices, planes, width = field.shape
    parts = 4 if width % (4 * LANES) == 0 else 1
    return pl.pallas_call(
        first_kernel,
        in_specs=[SMEM, SMEM, pl.BlockSpec(memory_space=pl.ANY)],
        scratch_shapes=[
            pltpu.VMEM((slices, planes, width + 2 * LANES), jnp.float32),
            pltpu.SemaphoreType.DMA((parts,)),
        ],
        **outputs_of(field.shape),
    )(step, mass, field)


def next_relax(core, step, mass, own, other, low, high, psi):
    slices, planes, width = psi.shape
    return pl.pallas_call(
        next_kernel,
        in_specs=[SMEM] * 3 + [VMEM] * 5,
        scratch_shapes=[pltpu.VMEM((slices, planes, width + 2 * LANES), jnp.float32)],
        **outputs_of(psi.shape),
    )(core, step, mass, own, other, low, high, psi)


class Loop:
    def __init__(self, mass, slices):
        self.devices = lax.axis_size("tm")
        self.me = lax.axis_index("tm")
        self.rate = 2.0 * jnp.arcsinh(0.5 * mass) * slices
        self.levels = self.devices.bit_length() - 1
        assert self.devices == 1 << self.levels

    def swap(self, array, offset):
        return lax.ppermute(array, "tm", [(i, i ^ offset) for i in range(self.devices)])

    def rho(self, level):
        return jnp.exp(-self.rate * (1 << level))

    def is_left(self, level):
        return (self.me >> level) & 1 == 0

    def merge(self, mine, theirs, level):
        left, rho = self.is_left(level), self.rho(level)
        ours, others = jnp.where(left, rho, 1.0), jnp.where(left, 1.0, rho)
        return jnp.stack([ours * mine[0] + others * theirs[0], others * mine[1] + ours * theirs[1]])

    def down(self, mine, theirs, both, level):
        left, rho = self.is_left(level), self.rho(level)
        before = jnp.where(left, both[0], theirs[0] + rho * both[0])
        after = jnp.where(left, theirs[1] + rho * both[1], both[1])
        return jnp.stack([before, after])

    def down_other(self, mine, theirs, both, level):
        left, rho = self.is_left(level), self.rho(level)
        before = jnp.where(left, mine[0] + rho * both[0], both[0])
        after = jnp.where(left, both[1], mine[1] + rho * both[1])
        return jnp.stack([before, after])

    def solve(self, ends):
        half = ends.shape[1] // 2
        bit = self.me & 1
        mine0 = lax.dynamic_slice_in_dim(ends, bit * half, half, 1)
        theirs0 = self.swap(lax.dynamic_slice_in_dim(ends, (1 - bit) * half, half, 1), 1)
        chip = self.merge(mine0, theirs0, 0)

        group = (self.me >> 1) & 3
        quarter = half // 4

        def part(k):
            return lax.dynamic_slice_in_dim(chip, (group ^ k) * quarter, quarter, 1)

        a0 = part(0)
        a1, a2, a3 = (self.swap(part(k), 2 * k) for k in (1, 2, 3))
        near, far = self.merge(a0, a1, 1), self.merge(a2, a3, 1)
        arc = self.merge(near, far, 2)
        stack = []
        for level in range(3, self.levels):
            theirs = self.swap(arc, 1 << level)
            stack.append((arc, theirs, level))
            arc = self.merge(arc, theirs, level)
        enters = arc / (1.0 - self.rho(self.levels))
        for mine, theirs, level in reversed(stack):
            enters = self.down(mine, theirs, enters, level)
        enters_near = self.down(near, far, enters, 2)
        enters_far = self.down_other(near, far, enters, 2)
        p0 = self.down(a0, a1, enters_near, 1)
        p1 = self.down_other(a0, a1, enters_near, 1)
        p2 = self.down(a2, a3, enters_far, 1)
        p3 = self.down_other(a2, a3, enters_far, 1)
        back = jnp.stack([p0] + [self.swap(p, 2 * k) for k, p in ((1, p1), (2, p2), (3, p3))])
        chip_enters = jnp.concatenate(
            [lax.dynamic_index_in_dim(back, group ^ k, 0, keepdims=False) for k in range(4)], axis=1
        )
        own = self.down(mine0, theirs0, chip_enters, 0)
        other = self.swap(self.down_other(mine0, theirs0, chip_enters, 0), 1)
        return own, other


class Planes:
    def __init__(self, planes):
        self.planes = planes
        self.devices = lax.axis_size("space")
        self.me = lax.axis_index("space")
        self.rounds = [p for p in (0, 1) if p + 1 < self.devices]

    def row(self, parity):
        return jnp.where(self.me % 2 == parity, self.planes - 1, 0)

    def exchange(self, rows):
        got = []
        for parity, given in zip(self.rounds, rows):
            low = range(parity, self.devices - 1, 2)
            got.append(lax.ppermute(given, "space", [(i, i + 1) for i in low] + [(i + 1, i) for i in low]))
        return got


def on_device(field, step, mass):
    slices, planes, width = field.shape
    loop = Loop(mass[0], slices)
    sides = Planes(planes)
    r, amplitude = decay(mass[0])
    rate = 2.0 * jnp.arcsinh(0.5 * mass[0])
    times = jnp.arange(slices).astype(jnp.float32)
    from_start = jnp.exp(-rate * times)
    from_end = from_start[::-1]
    green = step[0] * amplitude * jnp.exp(-rate * jnp.abs(times[:, None] - times[None, :]))
    weights = step[0] * amplitude * jnp.stack([from_end, from_start])
    core = (loop.me & 1).astype(jnp.int32).reshape(1)
    half = planes // 2

    def edge_terms(ends, halos):
        row = lax.broadcasted_iota(jnp.int32, (1, planes, 1), 1)
        low = high = jnp.zeros((slices, width), jnp.float32)
        for parity, halo in zip(sides.rounds, halos):
            touching = sides.row(parity)
            sums = jnp.sum(weights[:, :, None] * halo[None], axis=1)
            ends = ends - jnp.where(row == touching, sums[:, None, :], 0.0)
            term = jnp.dot(green, halo, precision=lax.Precision.HIGHEST)
            low = low + jnp.where(touching == 0, term, 0.0)
            high = high + jnp.where(touching == 0, 0.0, term)
        return ends, low, high

    def entering(own, other):
        mine = core[0] == 0
        return jnp.concatenate([jnp.where(mine, own, other), jnp.where(mine, other, own)], axis=1)

    given = [lax.dynamic_index_in_dim(field, sides.row(p), 1, keepdims=False) for p in sides.rounds]
    halos = sides.exchange(given)
    psi, ends = first_relax(field, step, mass)
    for turn in range(ITERS):
        ends, low, high = edge_terms(ends, halos)
        own, other = loop.solve(ends)
        both = entering(own, other)
        if turn < ITERS - 1:
            given = []
            for parity in sides.rounds:
                at = sides.row(parity)
                flux = lax.dynamic_index_in_dim(both, at, 1, keepdims=False)
                edge = lax.dynamic_index_in_dim(psi, at, 1, keepdims=False) + jnp.where(at == 0, low, high)
                edge = edge - (r * from_start)[:, None] * flux[0] - (r * from_end)[:, None] * flux[1]
                given.append(edge)
            halos = sides.exchange(given)
            psi, ends = next_relax(core, step, mass, own, other, low, high, psi)
    row = lax.broadcasted_iota(jnp.int32, (1, planes, 1), 1)
    field = psi - (r * from_start)[:, None, None] * both[0] - (r * from_end)[:, None, None] * both[1]
    field = field + jnp.where(row == 0, low[:, None, :], 0.0) + jnp.where(row == planes - 1, high[:, None, :], 0.0)
    return field


def solution(mesh):
    return jax.shard_map(
        on_device,
        mesh=mesh,
        in_specs=(P("tm", "space", None), P(), P()),
        out_specs=P("tm", "space", None),
        check_vma=False,
    )
```

```python
import functools

import jax
import jax.numpy as jnp
from jax import lax
from jax.experimental import pallas as pl
from jax.experimental.pallas import tpu as pltpu
from jax.sharding import PartitionSpec as P

NZ = 32
ITERS = 2

LANES = 128
ROWS = 8


def decay(mass):
    root = jnp.sqrt(1.0 + 0.25 * mass * mass)
    return 1.0 + 0.5 * mass * mass - mass * root, 0.5 / (mass * root)


def relax(phi, step_ref, mass_ref, psi_ref, ends_ref, edges_ref):
    slices, planes, width = psi_ref.shape
    blocks = planes // ROWS
    lane = lax.broadcasted_iota(jnp.int32, (ROWS, LANES), 1)
    row = lax.broadcasted_iota(jnp.int32, (ROWS, LANES), 0)
    mass = jnp.full((ROWS, LANES), mass_ref[0], jnp.float32)
    step = jnp.full((ROWS, LANES), step_ref[0], jnp.float32)
    r, amplitude = decay(mass)
    scale = step * amplitude
    c1, c2, c3 = scale * (7.0 - mass * mass), -0.9 * scale, 0.25 * scale
    keep = 1.0 - step
    first_z, last_z = lane % NZ == 0, lane % NZ == NZ - 1
    first_row, last_row = row == 0, row == ROWS - 1
    head, tail = lane < NZ, lane >= LANES - NZ
    zero = jnp.zeros((ROWS, LANES), jnp.float32)

    def at(t, i, start):
        return phi[t, ROWS * i : ROWS * (i + 1), pl.ds(start, LANES)]

    def tile(j, carry):
        start = pl.multiple_of((j + 1) * LANES, LANES)
        out = pl.ds(pl.multiple_of(j * LANES, LANES), LANES)
        for i in range(blocks):
            force = [None] * slices
            for k in range(slices):
                t = k // 2 if k % 2 == 0 else slices - 1 - k // 2
                v = at(t, i, start)
                before = zero if i == 0 else at(t, i - 1, start)
                after = zero if i == blocks - 1 else at(t, i + 1, start)
                total = pltpu.roll(jnp.where(last_row, before, v), 1, 0)
                total = total + pltpu.roll(jnp.where(first_row, after, v), ROWS - 1, 0)
                total = total + jnp.where(first_z, 0.0, pltpu.roll(v, 1, 1))
                total = total + jnp.where(last_z, 0.0, pltpu.roll(v, LANES - 1, 1))
                total = total + pltpu.roll(jnp.where(tail, at(t, i, start - LANES), v), NZ, 1)
                total = total + pltpu.roll(jnp.where(head, at(t, i, start + LANES), v), LANES - NZ, 1)
                force[t] = v * (c1 + v * (c2 + c3 * v)) - scale * total
            forward, backward = [None] * slices, [None] * slices
            a, b = force[0], force[-1]
            forward[0], backward[-1] = None, b
            for t in range(1, slices):
                forward[t] = r * a
                a = force[t] + forward[t]
                s = slices - 1 - t
                b = force[s] + r * b
                backward[s] = b
            rows = slice(ROWS * i, ROWS * (i + 1))
            ends_ref[0, rows, out] = a
            ends_ref[1, rows, out] = b
            for t in range(slices):
                local = backward[t] if t == 0 else forward[t] + backward[t]
                value = keep * at(t, i, start) - local
                psi_ref[t, rows, out] = value
                if i == 0:
                    edges_ref[0, t : t + 1, out] = value[:1]
                if i == blocks - 1:
                    edges_ref[1, t : t + 1, out] = value[ROWS - 1 :]
        return carry

    lax.fori_loop(0, width // LANES, tile, 0)


def clear_guards(phi):
    slices, planes, width = phi.shape
    guard = jnp.zeros((slices, planes, LANES), jnp.float32)
    phi[:, :, :LANES] = guard
    phi[:, :, width - LANES :] = guard


def load_kernel(field_ref, phi_ref, edges_ref, sems):
    slices, planes, padded = phi_ref.shape
    width = padded - 2 * LANES
    parts = sems.shape[0]
    part = planes // parts
    copies = []
    for n in range(parts):
        copies.append(
            pltpu.make_async_copy(
                field_ref.at[:, n * part : (n + 1) * part, :],
                phi_ref.at[:, n * part : (n + 1) * part, LANES : LANES + width],
                sems.at[n],
            )
        )
        copies[-1].start()
    clear_guards(phi_ref)
    for copy in copies:
        copy.wait()
    for t in range(slices):
        edges_ref[0, t : t + 1, :] = phi_ref[t, 0:1, LANES : LANES + width]
        edges_ref[1, t : t + 1, :] = phi_ref[t, planes - 1 : planes, LANES : LANES + width]


def first_kernel(step_ref, mass_ref, phi_ref, psi_ref, ends_ref, edges_ref):
    relax(phi_ref, step_ref, mass_ref, psi_ref, ends_ref, edges_ref)


def entered(half_ref, mass_ref, own_ref, other_ref, low_ref, high_ref, old_ref, new_ref, offset, done):
    slices, planes, width = old_ref.shape
    blocks = planes // ROWS
    mass = jnp.full((ROWS, LANES), mass_ref[0], jnp.float32)
    r, _ = decay(mass)
    inverse = 1.0 / r
    last = r
    for _ in range(slices - 1):
        last = last * r
    row = lax.broadcasted_iota(jnp.int32, (ROWS, LANES), 0)
    for i in range(blocks):
        rows = slice(ROWS * i, ROWS * (i + 1))
        half = 2 * i // blocks
        place = slice(ROWS * i - half * planes // 2, ROWS * (i + 1) - half * planes // 2)
        mine = half_ref[0] == half

        def tile(j, carry):
            lanes = pl.ds(pl.multiple_of(j * LANES, LANES), LANES)
            inner = pl.ds(pl.multiple_of(j * LANES + offset, LANES), LANES)
            p = jnp.where(mine, own_ref[0, place, lanes], other_ref[0, place, lanes]) * r
            q = jnp.where(mine, own_ref[1, place, lanes], other_ref[1, place, lanes]) * last
            for t in range(slices):
                value = old_ref[t, rows, lanes] - p - q
                if i == 0:
                    value = value + jnp.where(row == 0, low_ref[t : t + 1, lanes], 0.0)
                if i == blocks - 1:
                    value = value + jnp.where(row == ROWS - 1, high_ref[t : t + 1, lanes], 0.0)
                new_ref[t, rows, inner] = value
                p, q = p * r, q * inverse
            return carry

        lax.fori_loop(0, width // LANES, tile, 0)
        done(i)


def next_kernel(
    half_ref, step_ref, mass_ref, own_ref, other_ref, low_ref, high_ref, old_ref, psi_ref, ends_ref, edges_ref, phi
):
    clear_guards(phi)
    entered(half_ref, mass_ref, own_ref, other_ref, low_ref, high_ref, old_ref, phi, LANES, lambda i: None)
    relax(phi, step_ref, mass_ref, psi_ref, ends_ref, edges_ref)


def last_kernel(half_ref, mass_ref, own_ref, other_ref, low_ref, high_ref, old_ref, out_ref, stage, sems):
    copies = []

    def send(i):
        rows = slice(ROWS * i, ROWS * (i + 1))
        copies.append(pltpu.make_async_copy(stage.at[:, rows, :], out_ref.at[:, rows, :], sems.at[i]))
        copies[-1].start()

    entered(half_ref, mass_ref, own_ref, other_ref, low_ref, high_ref, old_ref, stage, 0, send)
    for copy in copies:
        copy.wait()


VMEM = pl.BlockSpec(memory_space=pltpu.VMEM)
SMEM = pl.BlockSpec(memory_space=pltpu.SMEM)
PARAMS = pltpu.CompilerParams(vmem_limit_bytes=24 * 2**20)


def in_vmem(array):
    return pltpu.with_memory_space_constraint(array, pltpu.VMEM)


def in_hbm(array):
    return pltpu.with_memory_space_constraint(array, pltpu.HBM)


def vmem(shape):
    return pltpu.VMEM(shape, jnp.float32)


def hbm(shape):
    return pltpu.HBM(shape, jnp.float32)


def cost(shape, flops):
    size = shape[0] * shape[1] * shape[2]
    return pl.CostEstimate(flops=flops * size, bytes_accessed=8 * size, transcendentals=0)


def relaxed(shape):
    slices, planes, width = shape
    return dict(
        out_shape=(
            vmem(shape),
            vmem((2, planes, width)),
            vmem((2, slices, width)),
        ),
        out_specs=(VMEM, VMEM, VMEM),
        compiler_params=PARAMS,
        cost_estimate=cost(shape, 30),
    )


def load(field):
    slices, planes, width = field.shape
    parts = planes // ROWS
    return pl.pallas_call(
        load_kernel,
        in_specs=[pl.BlockSpec(memory_space=pltpu.HBM)],
        out_shape=(
            vmem((slices, planes, width + 2 * LANES)),
            vmem((2, slices, width)),
        ),
        out_specs=(VMEM, VMEM),
        scratch_shapes=[pltpu.SemaphoreType.DMA((parts,))],
        compiler_params=PARAMS,
        cost_estimate=cost(field.shape, 1),
    )(in_hbm(field))


def first_relax(shape, phi, step, mass):
    return pl.pallas_call(first_kernel, in_specs=[SMEM, SMEM, VMEM], **relaxed(shape))(step, mass, in_vmem(phi))


def next_relax(half, step, mass, own, other, low, high, psi):
    slices, planes, width = psi.shape
    return pl.pallas_call(
        next_kernel,
        in_specs=[SMEM] * 3 + [VMEM] * 5,
        scratch_shapes=[pltpu.VMEM((slices, planes, width + 2 * LANES), jnp.float32)],
        **relaxed(psi.shape),
    )(half, step, mass, own, other, low, high, in_vmem(psi))


def last_step(half, mass, own, other, low, high, psi):
    slices, planes, width = psi.shape
    return pl.pallas_call(
        last_kernel,
        in_specs=[SMEM] * 2 + [VMEM] * 5,
        out_shape=hbm(psi.shape),
        out_specs=pl.BlockSpec(memory_space=pltpu.HBM),
        scratch_shapes=[pltpu.VMEM(psi.shape, jnp.float32), pltpu.SemaphoreType.DMA((planes // ROWS,))],
        compiler_params=PARAMS,
        cost_estimate=cost(psi.shape, 6),
    )(half, mass, own, other, low, high, in_vmem(psi))


class Loop:
    def __init__(self, mass, slices):
        self.devices = lax.axis_size("tm")
        self.me = lax.axis_index("tm")
        self.rate = 2.0 * jnp.arcsinh(0.5 * mass) * slices
        self.levels = self.devices.bit_length() - 1
        self.half = functools.reduce(jnp.bitwise_xor, [self.me >> k for k in range(self.levels)]) & 1
        assert self.devices == 1 << self.levels

    def swap(self, array, offset):
        offset = 2 * offset | offset.bit_count() & 1
        return self.exchange(array, offset)

    def exchange(self, array, offset):
        return lax.ppermute(array, "tm", [(i, i ^ offset) for i in range(self.devices)])

    def rho(self, level):
        return jnp.exp(-self.rate * (1 << level))

    def is_left(self, level):
        return (self.me >> level) & 1 == 0

    def merge(self, mine, theirs, level):
        left, rho = self.is_left(level), self.rho(level)
        ours, others = jnp.where(left, rho, 1.0), jnp.where(left, 1.0, rho)
        return jnp.stack([ours * mine[0] + others * theirs[0], others * mine[1] + ours * theirs[1]])

    def down(self, mine, theirs, both, level):
        left, rho = self.is_left(level), self.rho(level)
        before = jnp.where(left, both[0], theirs[0] + rho * both[0])
        after = jnp.where(left, theirs[1] + rho * both[1], both[1])
        return jnp.stack([before, after])

    def down_other(self, mine, theirs, both, level):
        left, rho = self.is_left(level), self.rho(level)
        before = jnp.where(left, mine[0] + rho * both[0], both[0])
        after = jnp.where(left, both[1], mine[1] + rho * both[1])
        return jnp.stack([before, after])

    def solve(self, ends):
        half = ends.shape[1] // 2
        bit = self.half
        mine0 = lax.dynamic_slice_in_dim(ends, bit * half, half, 1)
        theirs0 = self.exchange(lax.dynamic_slice_in_dim(ends, (1 - bit) * half, half, 1), 1)
        chip = self.merge(mine0, theirs0, 0)

        group = (self.me >> 1) & 3
        quarter = half // 4

        def part(k):
            return lax.dynamic_slice_in_dim(chip, (group ^ k) * quarter, quarter, 1)

        a0 = part(0)
        a1, a2, a3 = (self.swap(part(k), k) for k in (1, 2, 3))
        near, far = self.merge(a0, a1, 1), self.merge(a2, a3, 1)
        arc = self.merge(near, far, 2)
        stack = []
        for level in range(3, self.levels):
            theirs = self.swap(arc, 1 << level - 1)
            stack.append((arc, theirs, level))
            arc = self.merge(arc, theirs, level)
        enters = arc / (1.0 - self.rho(self.levels))
        for mine, theirs, level in reversed(stack):
            enters = self.down(mine, theirs, enters, level)
        enters_near = self.down(near, far, enters, 2)
        enters_far = self.down_other(near, far, enters, 2)
        p0 = self.down(a0, a1, enters_near, 1)
        p1 = self.down_other(a0, a1, enters_near, 1)
        p2 = self.down(a2, a3, enters_far, 1)
        p3 = self.down_other(a2, a3, enters_far, 1)
        back = jnp.stack([p0] + [self.swap(p, k) for k, p in ((1, p1), (2, p2), (3, p3))])
        chip_enters = jnp.concatenate(
            [lax.dynamic_index_in_dim(back, group ^ k, 0, keepdims=False) for k in range(4)], axis=1
        )
        own = self.down(mine0, theirs0, chip_enters, 0)
        other = self.exchange(self.down_other(mine0, theirs0, chip_enters, 0), 1)
        return own, other


class Planes:
    def __init__(self, planes):
        self.planes = planes
        self.devices = lax.axis_size("space")
        self.me = lax.axis_index("space")
        self.rounds = [p for p in (0, 1) if p + 1 < self.devices]

    def row(self, parity):
        return jnp.where(self.me % 2 == parity, self.planes - 1, 0)

    def exchange(self, rows):
        got = []
        for parity, given in zip(self.rounds, rows):
            low = range(parity, self.devices - 1, 2)
            got.append(lax.ppermute(given, "space", [(i, i + 1) for i in low] + [(i + 1, i) for i in low]))
        return got


def on_device(field, step, mass):
    slices, planes, width = field.shape
    loop = Loop(mass[0], slices)
    sides = Planes(planes)
    r, amplitude = decay(mass[0])
    rate = 2.0 * jnp.arcsinh(0.5 * mass[0])
    times = jnp.arange(slices).astype(jnp.float32)
    from_start = jnp.exp(-rate * times)
    from_end = from_start[::-1]
    green = step[0] * amplitude * jnp.exp(-rate * jnp.abs(times[:, None] - times[None, :]))
    weights = step[0] * amplitude * jnp.stack([from_end, from_start])
    half = loop.half.astype(jnp.int32).reshape(1)

    def edge_terms(ends, halos):
        row = lax.broadcasted_iota(jnp.int32, (1, planes, 1), 1)
        low = high = jnp.zeros((slices, width), jnp.float32)
        for parity, halo in zip(sides.rounds, halos):
            touching = sides.row(parity)
            sums = jnp.sum(weights[:, :, None] * halo[None], axis=1)
            ends = ends - jnp.where(row == touching, sums[:, None, :], 0.0)
            term = jnp.dot(green, halo, precision=lax.Precision.HIGHEST)
            low = low + jnp.where(touching == 0, term, 0.0)
            high = high + jnp.where(touching == 0, 0.0, term)
        return ends, low, high

    def give(edges):
        return sides.exchange([jnp.where(sides.row(p) == 0, edges[0], edges[1]) for p in sides.rounds])

    phi, edges = load(field)
    halos = give(edges)
    psi, ends, edges = first_relax(field.shape, phi, step, mass)
    for turn in range(ITERS):
        ends, low, high = edge_terms(ends, halos)
        own, other = loop.solve(ends)
        if turn < ITERS - 1:
            first = jnp.where(loop.half == 0, own[:, 0], other[:, 0])
            last = jnp.where(loop.half == 1, own[:, -1], other[:, -1])
            entering = [
                (r * from_start)[:, None] * flux[0] + (r * from_end)[:, None] * flux[1] for flux in (first, last)
            ]
            halos = give((edges[0] + low - entering[0], edges[1] + high - entering[1]))
            psi, ends, edges = next_relax(half, step, mass, own, other, low, high, psi)
    return last_step(half, mass, own, other, low, high, psi)


def solution(mesh):
    return jax.shard_map(
        on_device,
        mesh=mesh,
        in_specs=(P("tm", "space", None), P(), P()),
        out_specs=P("tm", "space", None),
        check_vma=False,
    )
```

```python
import functools

import jax
import jax.numpy as jnp
from jax import lax
from jax.experimental import pallas as pl
from jax.experimental.pallas import tpu as pltpu
from jax.sharding import PartitionSpec as P

NZ = 32
ITERS = 2

LANES = 128
ROWS = 8
TILE = (ROWS, LANES)
UNROLL = 4

DECAY, SCALE, LINEAR, SQUARE, CUBE, KEEP, WEIGHTS = range(7)


def decay(mass):
    root = jnp.sqrt(1.0 + 0.25 * mass * mass)
    return 1.0 + 0.5 * mass * mass - mass * root, 0.5 / (mass * root)


def fill_table(scalars, table, slices):
    step, mass = jnp.full(TILE, scalars[0], jnp.float32), jnp.full(TILE, scalars[1], jnp.float32)
    r, amplitude = decay(mass)
    scale = step * amplitude
    table[DECAY], table[SCALE], table[KEEP] = r, scale, 1.0 - step
    table[LINEAR], table[SQUARE], table[CUBE] = scale * (7.0 - mass * mass), -0.9 * scale, 0.25 * scale
    powers = [jnp.ones(TILE, jnp.float32)]
    for _ in range(slices - 1):
        powers.append(powers[-1] * r)
    for k in range(slices // 2):
        table[WEIGHTS + 2 * k] = 0.5 * (powers[k] + powers[slices - 1 - k])
        table[WEIGHTS + 2 * k + 1] = 0.5 * (powers[k] - powers[slices - 1 - k])


def fill_wide(scalars, planes_ref, arcs_ref, levels):
    _, slices, width = planes_ref.shape

    def rate_of(shape):
        half = 0.5 * jnp.full(shape, scalars[1], jnp.float32)
        return 2.0 * jnp.log1p(half + half * half / (1.0 + jnp.sqrt(1.0 + half * half)))

    shape = (slices, LANES)
    rate = rate_of(shape)
    t = lax.broadcasted_iota(jnp.int32, shape, 0).astype(jnp.float32)
    mass = jnp.full(shape, scalars[1], jnp.float32)
    scale = jnp.full(shape, scalars[0], jnp.float32) * decay(mass)[1]
    start, end = jnp.exp(-rate * t), jnp.exp(-rate * (slices - 1 - t))
    r = jnp.exp(-rate)
    values = (r * start, r * end, scale * end, scale * start)
    row = lax.broadcasted_iota(jnp.int32, TILE, 0)
    rate = rate_of(TILE)
    arcs = jnp.zeros(TILE, jnp.float32)
    for level in range(levels):
        arcs = jnp.where(row == level, jnp.exp(-rate * (slices << level)), arcs)
    arcs = jnp.where(row == levels, 1.0 / (1.0 - jnp.exp(-rate * (slices << levels))), arcs)

    def tile(j, carry):
        for n, value in enumerate(values):
            planes_ref[n, :, tile_at(j)] = value
        arcs_ref[:, tile_at(j)] = arcs
        return carry

    lax.fori_loop(0, width // LANES, tile, 0)


def rows_of(i):
    return slice(ROWS * i, ROWS * (i + 1))


def tile_at(j, offset=0):
    return pl.ds(pl.multiple_of(j * LANES + offset, LANES), LANES)


class Masks:
    def __init__(self):
        lane = lax.broadcasted_iota(jnp.int32, TILE, 1)
        row = lax.broadcasted_iota(jnp.int32, TILE, 0)
        self.first_z, self.last_z = lane % NZ == 0, lane % NZ == NZ - 1
        self.first_row, self.last_row = row == 0, row == ROWS - 1
        self.head, self.tail = lane < NZ, lane >= LANES - NZ


def neighbours(masks, v, before, after, left, right):
    total = pltpu.roll(jnp.where(masks.last_row, before, v), 1, 0)
    total = total + pltpu.roll(jnp.where(masks.first_row, after, v), ROWS - 1, 0)
    total = total + jnp.where(masks.first_z, 0.0, pltpu.roll(v, 1, 1))
    total = total + jnp.where(masks.last_z, 0.0, pltpu.roll(v, LANES - 1, 1))
    total = total + pltpu.roll(jnp.where(masks.tail, left, v), NZ, 1)
    return total + pltpu.roll(jnp.where(masks.head, right, v), LANES - NZ, 1)


def entering_tile(table, half_ref, own_ref, other_ref, i, blocks, lanes):
    half = 2 * i // blocks
    place = rows_of(i - half * blocks // 2)
    mine = half_ref[0] == half
    p = jnp.where(mine, own_ref[0, place, lanes], other_ref[0, place, lanes])
    q = jnp.where(mine, own_ref[1, place, lanes], other_ref[1, place, lanes])
    r = table[DECAY]
    return r * (p + q), r * (p - q)


def entered_pair(table, both, old, k, i, lanes):
    v, w = old[k, rows_of(i), lanes], old[old.shape[0] - 1 - k, rows_of(i), lanes]
    if both is None:
        return v, w
    even, odd = table[WEIGHTS + 2 * k] * both[0], table[WEIGHTS + 2 * k + 1] * both[1]
    return v - (even + odd), w - (even - odd)


def sum_tiles(table, enter, old, ends_ref, sums, tiles):
    slices, planes, _ = old.shape
    blocks = planes // ROWS

    def tile(j, carry):
        lanes = tile_at(j)
        for i in range(blocks):
            both = enter(i, lanes) if enter else None
            for k in range(slices // 2):
                v, w = entered_pair(table, both, old, k, i, lanes)
                f = v * v * (table[SQUARE] + table[CUBE] * v)
                g = w * w * (table[SQUARE] + table[CUBE] * w)
                a, b = table[WEIGHTS + 2 * k], table[WEIGHTS + 2 * k + 1]
                terms = (a * (v + w), b * (v - w), a * (f + g), b * (f - g))
                total = terms if k == 0 else tuple(x + y for x, y in zip(total, terms))
            for n, (field, force) in enumerate(
                ((total[0] - total[1], total[2] - total[3]), (total[0] + total[1], total[2] + total[3]))
            ):
                sums[n, rows_of(i), tile_at(j, LANES)] = field
                ends_ref[n, rows_of(i), lanes] = force + table[LINEAR] * field
        return carry

    lax.fori_loop(tiles[0], tiles[1], tile, 0, unroll=UNROLL)


def finish_sums(table, ends_ref, sums):
    _, planes, width = ends_ref.shape
    blocks = planes // ROWS
    masks = Masks()
    zero = jnp.zeros(TILE, jnp.float32)

    def tile(j, carry):
        for n in range(2):
            at = lambda i, side: sums[n, rows_of(i), tile_at(j, (1 + side) * LANES)]
            for i in range(blocks):
                before = zero if i == 0 else at(i - 1, 0)
                after = zero if i == blocks - 1 else at(i + 1, 0)
                total = neighbours(masks, at(i, 0), before, after, at(i, -1), at(i, 1))
                ends_ref[n, rows_of(i), tile_at(j)] -= table[SCALE] * total
        return carry

    lax.fori_loop(0, width // LANES, tile, 0, unroll=UNROLL)


def clear_guards(ref):
    lead, planes, width = ref.shape
    guard = jnp.zeros((lead, planes, LANES), jnp.float32)
    ref[:, :, :LANES] = guard
    ref[:, :, width - LANES :] = guard


def lane_parts(width, parts):
    part = width // parts
    return [slice(n * part, (n + 1) * part) for n in range(parts)]


def tiles_of(lanes):
    return lanes.start // LANES, lanes.stop // LANES


def start_reads(source, target, parts, sems, offset=0):
    reads = []
    for n, lanes in enumerate(parts):
        there = slice(lanes.start + offset, lanes.stop + offset)
        reads.append(pltpu.make_async_copy(source.at[:, :, lanes], target.at[:, :, there], sems.at[n]))
        reads[-1].start()
    return reads


def sum_parts(table, enter, old_ref, old, ends_ref, sums, parts, reads):
    for lanes, read in zip(parts, reads):
        read.wait()
        sum_tiles(table, enter, old, ends_ref, sums, tiles_of(lanes))
    finish_sums(table, ends_ref, sums)


def first_sums_kernel(
    levels, step_ref, mass_ref, old_ref, ends_ref, table, planes_ref, arcs_ref, old, sums, sems
):
    parts = lane_parts(old.shape[-1], sems.shape[0])
    reads = start_reads(old_ref, old, parts, sems)
    clear_guards(sums)
    values = step_ref[0], mass_ref[0]
    fill_table(values, table, old.shape[0])
    fill_wide(values, planes_ref, arcs_ref, levels)
    sum_parts(table, None, old_ref, old, ends_ref, sums, parts, reads)


def next_sums_kernel(half_ref, table, own_ref, other_ref, old_ref, ends_ref, old, sums, sems):
    parts = lane_parts(old.shape[-1], sems.shape[0])
    reads = start_reads(old_ref, old, parts, sems)
    clear_guards(sums)
    blocks = old.shape[1] // ROWS

    def enter(i, lanes):
        return entering_tile(table, half_ref, own_ref, other_ref, i, blocks, lanes)

    sum_parts(table, enter, old_ref, old, ends_ref, sums, parts, reads)


def relax_tiles(table, masks, phi, low_ref, high_ref, stage, edges_ref, tiles):
    slices, planes, _ = stage.shape
    blocks = planes // ROWS
    half = slices // 2

    def tile(j, carry):
        lanes = tile_at(j)
        for i in range(blocks):
            at = lambda t, i, side: phi[t, rows_of(i), tile_at(j, (1 + side) * LANES)]
            force = [None] * slices
            for n in range(slices):
                t = n // 2 if n % 2 == 0 else slices - 1 - n // 2
                v = at(t, i, 0)
                before = low_ref[t : t + 1, lanes] if i == 0 else at(t, i - 1, 0)
                after = high_ref[t : t + 1, lanes] if i == blocks - 1 else at(t, i + 1, 0)
                total = neighbours(masks, v, before, after, at(t, i, -1), at(t, i, 1))
                force[t] = v * (table[LINEAR] + v * (table[SQUARE] + table[CUBE] * v)) - table[SCALE] * total
            forward, backward = [None] * slices, [None] * slices
            a, b = force[0], force[-1]
            backward[-1] = b
            r = table[DECAY]
            for t in range(1, slices):
                forward[t] = r * a
                a = force[t] + forward[t]
                s = slices - 1 - t
                b = force[s] + r * b
                backward[s] = b
            for t in range(slices):
                local = backward[t] if t == 0 else forward[t] + backward[t]
                value = table[KEEP] * at(t, i, 0) - local
                stage[t, rows_of(i), lanes] = value
                if i == 0:
                    edges_ref[0, t : t + 1, lanes] = value[:1]
                if i == blocks - 1:
                    edges_ref[1, t : t + 1, lanes] = value[ROWS - 1 :]
        return carry

    lax.fori_loop(tiles[0], tiles[1], tile, 0, unroll=min(UNROLL, tiles[1] - tiles[0]))


def relax_piece(table, enter, low_ref, high_ref, old_ref, psi_ref, edges_ref, phi, stage, old, in_sems, out_sems, tiles):
    slices, planes, width = stage.shape
    blocks = planes // ROWS
    first, last = tiles
    middle = (first + last) // 2
    bounds = [max(first - 1, 0), middle + 1, min(last + 1, width // LANES)]
    parts = [slice(a * LANES, b * LANES) for a, b in zip(bounds, bounds[1:])]
    reads = start_reads(old_ref, old if enter else phi, parts, in_sems, 0 if enter else LANES)
    clear_guards(phi)
    masks = Masks()

    def arrive(n):
        reads[n].wait()
        if not enter:
            return

        def tile(j, carry):
            lanes, inner = tile_at(j), tile_at(j, LANES)
            for i in range(blocks):
                both = enter(i, lanes)
                for k in range(slices // 2):
                    v, w = entered_pair(table, both, old, k, i, lanes)
                    phi[k, rows_of(i), inner] = v
                    phi[slices - 1 - k, rows_of(i), inner] = w
            return carry

        lax.fori_loop(bounds[n], bounds[n + 1], tile, 0, unroll=True)

    writes = []
    for n, part in enumerate(((first, middle), (middle, last))):
        arrive(n)
        relax_tiles(table, masks, phi, low_ref, high_ref, stage, edges_ref, part)
        lanes = slice(part[0] * LANES, part[1] * LANES)
        writes.append(pltpu.make_async_copy(stage.at[:, :, lanes], psi_ref.at[:, :, lanes], out_sems.at[n]))
        writes[-1].start()
    for write in writes:
        write.wait()


def first_relax_kernel(tiles, table, low_ref, high_ref, old_ref, _, psi_ref, edges_ref, phi, stage, in_sems, out_sems):
    relax_piece(
        table, None, low_ref, high_ref, old_ref, psi_ref, edges_ref, phi, stage, None, in_sems, out_sems, tiles
    )


def next_relax_kernel(
    tiles, half_ref, table, own_ref, other_ref, low_ref, high_ref, old_ref, _,
    psi_ref, edges_ref, phi, stage, old, in_sems, out_sems,
):
    blocks = old.shape[1] // ROWS

    def enter(i, lanes):
        return entering_tile(table, half_ref, own_ref, other_ref, i, blocks, lanes)

    relax_piece(
        table, enter, low_ref, high_ref, old_ref, psi_ref, edges_ref, phi, stage, old, in_sems, out_sems, tiles
    )


def last_kernel(half_ref, table, own_ref, other_ref, old_ref, out_ref, old, stage, in_sems, out_sems):
    slices, planes, width = old.shape
    blocks = planes // ROWS
    parts = lane_parts(width, in_sems.shape[0])
    reads = start_reads(old_ref, old, parts, in_sems)
    writes = []

    def tile(j, carry):
        lanes = tile_at(j)
        for i in range(blocks):
            both = entering_tile(table, half_ref, own_ref, other_ref, i, blocks, lanes)
            for k in range(slices // 2):
                v, w = entered_pair(table, both, old, k, i, lanes)
                stage[k, rows_of(i), lanes] = v
                stage[slices - 1 - k, rows_of(i), lanes] = w
        return carry

    for n, lanes in enumerate(parts):
        reads[n].wait()
        lax.fori_loop(*tiles_of(lanes), tile, 0, unroll=UNROLL)
        writes.append(pltpu.make_async_copy(stage.at[:, :, lanes], out_ref.at[:, :, lanes], out_sems.at[n]))
        writes[-1].start()
    for write in writes:
        write.wait()


VMEM = pl.BlockSpec(memory_space=pltpu.VMEM)
SMEM = pl.BlockSpec(memory_space=pltpu.SMEM)
HBM = pl.BlockSpec(memory_space=pltpu.HBM)
PARAMS = pltpu.CompilerParams(vmem_limit_bytes=24 * 2**20)


def in_hbm(array):
    return pltpu.with_memory_space_constraint(array, pltpu.HBM)


def hbm(shape):
    return pltpu.HBM(shape, jnp.float32)


def f32(shape):
    return jax.ShapeDtypeStruct(shape, jnp.float32)


def padded(lead, shape):
    return pltpu.VMEM((lead, shape[1], shape[2] + 2 * LANES), jnp.float32)


def parts_of(width):
    return 4 if width % (4 * LANES) == 0 else 1


def cost(shape, flops):
    size = shape[0] * shape[1] * shape[2]
    return pl.CostEstimate(flops=flops * size, bytes_accessed=4 * size, transcendentals=0)


def first_sums(step, mass, field, levels):
    slices, planes, width = field.shape
    assert slices % 2 == 0 and levels < ROWS
    return pl.pallas_call(
        functools.partial(first_sums_kernel, levels),
        in_specs=[SMEM] * 2 + [HBM],
        out_shape=(
            f32((2, planes, width)),
            f32((WEIGHTS + slices, *TILE)),
            f32((4, slices, width)),
            f32((ROWS, width)),
        ),
        out_specs=(VMEM,) * 4,
        scratch_shapes=[
            pltpu.VMEM(field.shape, jnp.float32),
            padded(2, field.shape),
            pltpu.SemaphoreType.DMA((parts_of(width),)),
        ],
        compiler_params=PARAMS,
        cost_estimate=cost(field.shape, 12),
    )(step, mass, in_hbm(field))


def next_sums(half, table, own, other, psi):
    _, planes, width = psi.shape
    return pl.pallas_call(
        next_sums_kernel,
        in_specs=[SMEM] + [VMEM] * 3 + [HBM],
        out_shape=f32((2, planes, width)),
        out_specs=VMEM,
        scratch_shapes=[
            pltpu.VMEM(psi.shape, jnp.float32),
            padded(2, psi.shape),
            pltpu.SemaphoreType.DMA((parts_of(width),)),
        ],
        compiler_params=PARAMS,
        cost_estimate=cost(psi.shape, 16),
    )(half, table, own, other, in_hbm(psi))


def relax(tiles, terms, table, low, high, old, psi):
    slices, planes, width = old.shape
    if terms:
        half, own, other = terms
        kernel, operands, specs = next_relax_kernel, [half, table, own, other], [SMEM] + [VMEM] * 3
    else:
        kernel, operands, specs = first_relax_kernel, [table], [VMEM]
    operands += [low, high, in_hbm(old)]
    specs += [VMEM, VMEM, HBM]
    aliases = {}
    if psi is not None:
        operands.append(in_hbm(psi))
        specs.append(HBM)
        aliases = {len(operands) - 1: 0}

    def body(*refs):
        refs = list(refs)
        if psi is None:
            refs.insert(len(operands), None)
        kernel(tiles, *refs)

    return pl.pallas_call(
        body,
        in_specs=specs,
        out_shape=(hbm(old.shape), f32((2, slices, width))),
        out_specs=(HBM, VMEM),
        input_output_aliases=aliases,
        scratch_shapes=[padded(slices, old.shape), pltpu.VMEM(old.shape, jnp.float32)]
        + ([pltpu.VMEM(old.shape, jnp.float32)] if terms else [])
        + [pltpu.SemaphoreType.DMA((2,))] * 2,
        compiler_params=PARAMS,
        cost_estimate=cost((slices, planes, (tiles[1] - tiles[0]) * LANES), 40),
    )(*operands)


def last_step(half, table, own, other, psi):
    semaphores = pltpu.SemaphoreType.DMA((parts_of(psi.shape[-1]),))
    return pl.pallas_call(
        last_kernel,
        in_specs=[SMEM] + [VMEM] * 3 + [HBM],
        out_shape=hbm(psi.shape),
        out_specs=HBM,
        scratch_shapes=[pltpu.VMEM(psi.shape, jnp.float32)] * 2 + [semaphores] * 2,
        compiler_params=PARAMS,
        cost_estimate=cost(psi.shape, 6),
    )(half, table, own, other, in_hbm(psi))


class Loop:
    def __init__(self):
        self.devices = lax.axis_size("tm")
        self.me = lax.axis_index("tm")
        self.levels = self.devices.bit_length() - 1
        assert self.devices == 1 << self.levels and self.levels > 3

    def swap(self, array, offset):
        return lax.ppermute(array, "tm", [(i, i ^ offset) for i in range(self.devices)])

    def rho(self, level):
        return self.arcs[level : level + 1]

    def is_left(self, level):
        return (self.me >> level) & 1 == 0

    def merge(self, mine, theirs, level):
        left, rho = self.is_left(level), self.rho(level)
        ours, others = jnp.where(left, rho, 1.0), jnp.where(left, 1.0, rho)
        return jnp.stack([ours * mine[0] + others * theirs[0], others * mine[1] + ours * theirs[1]])

    def down(self, mine, theirs, both, level):
        left, rho = self.is_left(level), self.rho(level)
        before = jnp.where(left, both[0], theirs[0] + rho * both[0])
        after = jnp.where(left, theirs[1] + rho * both[1], both[1])
        return jnp.stack([before, after])

    def down_other(self, mine, theirs, both, level):
        left, rho = self.is_left(level), self.rho(level)
        before = jnp.where(left, mine[0] + rho * both[0], both[0])
        after = jnp.where(left, both[1], mine[1] + rho * both[1])
        return jnp.stack([before, after])

    def solve(self, ends, arcs, works):
        self.arcs = arcs
        half = ends.shape[1] // 2
        bit = self.me & 1
        mine0 = lax.dynamic_slice_in_dim(ends, bit * half, half, 1)
        theirs0 = self.swap(lax.dynamic_slice_in_dim(ends, (1 - bit) * half, half, 1), 1)
        chip = self.merge(mine0, theirs0, 0)

        group = (self.me >> 1) & 3
        quarter = half // 4

        def part(k):
            return lax.dynamic_slice_in_dim(chip, (group ^ k) * quarter, quarter, 1)

        a0 = part(0)
        received = [self.swap(part(k), 2 * k) for k in (1, 2, 3)]
        state = works[0](chip)
        (a1, a2, a3), state = lax.optimization_barrier((received, state))
        near, far = self.merge(a0, a1, 1), self.merge(a2, a3, 1)
        arc = self.merge(near, far, 2)
        stack = []
        for level in range(3, self.levels):
            theirs = self.swap(arc, 1 << level)
            if level == 3:
                state = works[1](arc, state)
                theirs, state = lax.optimization_barrier((theirs, state))
            stack.append((arc, theirs, level))
            arc = self.merge(arc, theirs, level)
        enters = arc * self.rho(self.levels)
        for mine, theirs, level in reversed(stack):
            enters = self.down(mine, theirs, enters, level)
        enters_near = self.down(near, far, enters, 2)
        enters_far = self.down_other(near, far, enters, 2)
        p0 = self.down(a0, a1, enters_near, 1)
        p1 = self.down_other(a0, a1, enters_near, 1)
        p2 = self.down(a2, a3, enters_far, 1)
        p3 = self.down_other(a2, a3, enters_far, 1)
        received = [self.swap(p, 2 * k) for k, p in ((1, p1), (2, p2), (3, p3))]
        state = works[2](enters, state)
        received, state = lax.optimization_barrier((received, state))
        back = jnp.stack([p0] + received)
        chip_enters = jnp.concatenate(
            [lax.dynamic_index_in_dim(back, group ^ k, 0, keepdims=False) for k in range(4)], axis=1
        )
        own = self.down(mine0, theirs0, chip_enters, 0)
        other = self.swap(self.down_other(mine0, theirs0, chip_enters, 0), 1)
        return own, other, state


class Planes:
    def __init__(self, planes):
        self.planes = planes
        self.devices = lax.axis_size("space")
        self.me = lax.axis_index("space")
        self.rounds = [p for p in (0, 1) if p + 1 < self.devices]

    def row(self, parity):
        return jnp.where(self.me % 2 == parity, self.planes - 1, 0)

    def exchange(self, first, last):
        low = high = jnp.zeros_like(first)
        for parity in self.rounds:
            given = jnp.where(self.row(parity) == 0, first, last)
            pairs = range(parity, self.devices - 1, 2)
            got = lax.ppermute(given, "space", [(i, i + 1) for i in pairs] + [(i + 1, i) for i in pairs])
            low = low + jnp.where(self.row(parity) == 0, got, 0.0)
            high = high + jnp.where(self.row(parity) == 0, 0.0, got)
        return low, high


def on_device(field, step, mass):
    _, planes, width = field.shape
    loop = Loop()
    sides = Planes(planes)
    half = (loop.me & 1).astype(jnp.int32).reshape(1)
    tiles = width // LANES
    bounds = [0, 3 * tiles // 8, 5 * tiles // 8, tiles]

    def after(array, *others):
        return lax.optimization_barrier((array, *others))[0]

    old, terms = field, None
    first, last = field[:, 0], field[:, -1]
    for turn in range(ITERS):
        low, high = sides.exchange(first, last)
        if turn == 0:
            ends, table, weights, arcs = first_sums(step, mass, old, loop.levels)
        else:
            ends = next_sums(half, table, *terms[1:], old)
        row = lax.broadcasted_iota(jnp.int32, (1, planes, 1), 1)
        for place, plane in ((0, low), (planes - 1, high)):
            sums = jnp.sum(weights[2:] * plane[None], axis=1)
            ends = ends - jnp.where(row == place, sums[:, None, :], 0.0)

        def work(n, ready, state=None, old=old, terms=terms, low=low, high=high):
            psi, edges = state or (None, [])
            psi, more = relax(bounds[n : n + 2], terms, after(table, ready), low, high, old, psi)
            return psi, edges + [more[..., bounds[n] * LANES : bounds[n + 1] * LANES]]

        works = [functools.partial(work, n) for n in range(3)]
        own, other, (old, edges) = loop.solve(ends, arcs, works)
        terms = (half, own, other)
        if turn < ITERS - 1:
            edges = jnp.concatenate(edges, axis=2)
            mine = half[0] == 0
            first, last = (
                edges[n] - weights[0] * flux[0] - weights[1] * flux[1]
                for n, flux in (
                    (0, jnp.where(mine, own[:, 0], other[:, 0])),
                    (1, jnp.where(mine, other[:, -1], own[:, -1])),
                )
            )
    return last_step(half, table, own, other, old)


def solution(mesh):
    return jax.shard_map(
        on_device,
        mesh=mesh,
        in_specs=(P("tm", "space", None), P(), P()),
        out_specs=P("tm", "space", None),
        check_vma=False,
    )
```

```python
import functools

import jax
import jax.numpy as jnp
from jax import lax
from jax.experimental import pallas as pl
from jax.experimental.pallas import tpu as pltpu
from jax.sharding import PartitionSpec as P

NZ = 32

LANES = 128
ROWS = 8
TILE = (ROWS, LANES)
UNROLL = 4
PARTS = 3

DECAY, SCALE, LINEAR, SQUARE, CUBE, KEEP, WEIGHTS = range(7)


def decay(mass):
    root = jnp.sqrt(1.0 + 0.25 * mass * mass)
    return 1.0 + 0.5 * mass * mass - mass * root, 0.5 / (mass * root)


def fill_table(scalars, table, slices):
    step, mass = jnp.full(TILE, scalars[0], jnp.float32), jnp.full(TILE, scalars[1], jnp.float32)
    r, amplitude = decay(mass)
    scale = step * amplitude
    table[DECAY], table[SCALE], table[KEEP] = r, scale, 1.0 - step
    table[LINEAR], table[SQUARE], table[CUBE] = scale * (7.0 - mass * mass), -0.9 * scale, 0.25 * scale
    powers = [jnp.ones(TILE, jnp.float32)]
    for _ in range(slices - 1):
        powers.append(powers[-1] * r)
    for k in range(slices // 2):
        table[WEIGHTS + 2 * k] = 0.5 * (powers[k] + powers[slices - 1 - k])
        table[WEIGHTS + 2 * k + 1] = 0.5 * (powers[k] - powers[slices - 1 - k])


def fill_wide(scalars, planes_ref, arcs_ref, levels):
    _, slices, width = planes_ref.shape

    def rate_of(shape):
        half = 0.5 * jnp.full(shape, scalars[1], jnp.float32)
        return 2.0 * jnp.log1p(half + half * half / (1.0 + jnp.sqrt(1.0 + half * half)))

    shape = (slices, LANES)
    rate = rate_of(shape)
    t = lax.broadcasted_iota(jnp.int32, shape, 0).astype(jnp.float32)
    mass = jnp.full(shape, scalars[1], jnp.float32)
    scale = jnp.full(shape, scalars[0], jnp.float32) * decay(mass)[1]
    start, end = jnp.exp(-rate * t), jnp.exp(-rate * (slices - 1 - t))
    r = jnp.exp(-rate)
    values = (r * start, r * end, scale * end, scale * start)
    row = lax.broadcasted_iota(jnp.int32, TILE, 0)
    rate = rate_of(TILE)
    arcs = jnp.zeros(TILE, jnp.float32)
    for level in range(levels):
        arcs = jnp.where(row == level, jnp.exp(-rate * (slices << level)), arcs)
    arcs = jnp.where(row == levels, 1.0 / (1.0 - jnp.exp(-rate * (slices << levels))), arcs)

    def tile(j, carry):
        for n, value in enumerate(values):
            planes_ref[n, :, tile_at(j)] = value
        arcs_ref[:, tile_at(j)] = arcs
        return carry

    lax.fori_loop(0, width // LANES, tile, 0)


def rows_of(i):
    return slice(ROWS * i, ROWS * (i + 1))


def tile_at(j, offset=0):
    return pl.ds(pl.multiple_of(j * LANES + offset, LANES), LANES)


class Masks:
    def __init__(self):
        lane = lax.broadcasted_iota(jnp.int32, TILE, 1)
        row = lax.broadcasted_iota(jnp.int32, TILE, 0)
        self.first_z, self.last_z = lane % NZ == 0, lane % NZ == NZ - 1
        self.first_row, self.last_row = row == 0, row == ROWS - 1
        self.head, self.tail = lane < NZ, lane >= LANES - NZ


def neighbours(masks, v, before, after, left, right):
    total = pltpu.roll(jnp.where(masks.last_row, before, v), 1, 0)
    total = total + pltpu.roll(jnp.where(masks.first_row, after, v), ROWS - 1, 0)
    total = total + jnp.where(masks.first_z, 0.0, pltpu.roll(v, 1, 1))
    total = total + jnp.where(masks.last_z, 0.0, pltpu.roll(v, LANES - 1, 1))
    total = total + pltpu.roll(jnp.where(masks.tail, left, v), NZ, 1)
    return total + pltpu.roll(jnp.where(masks.head, right, v), LANES - NZ, 1)


def entering_tile(table, half_ref, own_ref, other_ref, i, blocks, lanes):
    half = 2 * i // blocks
    place = rows_of(i - half * blocks // 2)
    mine = half_ref[0] == half
    p = jnp.where(mine, own_ref[0, place, lanes], other_ref[0, place, lanes])
    q = jnp.where(mine, own_ref[1, place, lanes], other_ref[1, place, lanes])
    r = table[DECAY]
    return r * (p + q), r * (p - q)


def entered_pair(table, both, old, k, i, place):
    v, w = old[k, rows_of(i), place], old[old.shape[0] - 1 - k, rows_of(i), place]
    if both is None:
        return v, w
    even, odd = table[WEIGHTS + 2 * k] * both[0], table[WEIGHTS + 2 * k + 1] * both[1]
    return v - (even + odd), w - (even - odd)


def sum_tiles(table, enter, old, ends_ref, sums, tiles):
    slices, planes, _ = old.shape
    blocks = planes // ROWS

    def tile(j, carry):
        lanes = tile_at(j)
        for i in range(blocks):
            both = enter(i, lanes) if enter else None
            for k in range(slices // 2):
                v, w = entered_pair(table, both, old, k, i, lanes)
                f = v * v * (table[SQUARE] + table[CUBE] * v)
                g = w * w * (table[SQUARE] + table[CUBE] * w)
                a, b = table[WEIGHTS + 2 * k], table[WEIGHTS + 2 * k + 1]
                terms = (a * (v + w), b * (v - w), a * (f + g), b * (f - g))
                total = terms if k == 0 else tuple(x + y for x, y in zip(total, terms))
            for n, (field, force) in enumerate(
                ((total[0] - total[1], total[2] - total[3]), (total[0] + total[1], total[2] + total[3]))
            ):
                sums[n, rows_of(i), tile_at(j, LANES)] = field
                ends_ref[n, rows_of(i), lanes] = force + table[LINEAR] * field
        return carry

    lax.fori_loop(tiles[0], tiles[1], tile, 0, unroll=UNROLL)


def finish_sums(table, ends_ref, sums):
    _, planes, width = ends_ref.shape
    blocks = planes // ROWS
    masks = Masks()
    zero = jnp.zeros(TILE, jnp.float32)

    def tile(j, carry):
        for n in range(2):
            at = lambda i, side: sums[n, rows_of(i), tile_at(j, (1 + side) * LANES)]
            for i in range(blocks):
                before = zero if i == 0 else at(i - 1, 0)
                after = zero if i == blocks - 1 else at(i + 1, 0)
                total = neighbours(masks, at(i, 0), before, after, at(i, -1), at(i, 1))
                ends_ref[n, rows_of(i), tile_at(j)] -= table[SCALE] * total
        return carry

    lax.fori_loop(0, width // LANES, tile, 0, unroll=UNROLL)


def clear_guards(ref):
    lead, planes, width = ref.shape
    guard = jnp.zeros((lead, planes, LANES), jnp.float32)
    ref[:, :, :LANES] = guard
    ref[:, :, width - LANES :] = guard


def bounds_of(width):
    tiles = width // LANES
    return [0, 3 * tiles // 8, 5 * tiles // 8, tiles]


def pieces_of(width):
    bounds = bounds_of(width)
    return list(zip(bounds, bounds[1:]))


def lanes_of(first, last):
    return slice(first * LANES, last * LANES)


def sum_parts(table, enter, source, ends_ref, old, sums, sems, prepare):
    tiles = ends_ref.shape[-1] // LANES
    count = sems.shape[0]
    reads = []
    for n in range(count):
        part = n * tiles // count, (n + 1) * tiles // count
        lanes = lanes_of(*part)
        reads.append((part, pltpu.make_async_copy(source.at[:, :, lanes], old.at[:, :, lanes], sems.at[n])))
        reads[-1][1].start()
    clear_guards(sums)
    prepare()
    for part, read in reads:
        read.wait()
        sum_tiles(table, enter, old, ends_ref, sums, part)
    finish_sums(table, ends_ref, sums)


def first_sums_kernel(
    levels, step_ref, mass_ref, old_ref, ends_ref, table, planes_ref, arcs_ref, old, sums, sems
):
    def prepare():
        values = step_ref[0], mass_ref[0]
        fill_table(values, table, old.shape[0])
        fill_wide(values, planes_ref, arcs_ref, levels)

    sum_parts(table, None, old_ref, ends_ref, old, sums, sems, prepare)


def next_sums_kernel(half_ref, table, own_ref, other_ref, old_ref, ends_ref, old, sums, sems):
    blocks = ends_ref.shape[1] // ROWS

    def enter(i, lanes):
        return entering_tile(table, half_ref, own_ref, other_ref, i, blocks, lanes)

    sum_parts(table, enter, old_ref, ends_ref, old, sums, sems, lambda: None)


def relax_tiles(table, masks, phi, low_ref, high_ref, psi_ref, edges_ref, tiles, start):
    slices, planes, _ = phi.shape
    blocks = planes // ROWS

    def tile(j, carry):
        lanes, place = tile_at(j), tile_at(j, -start * LANES)
        for i in range(blocks):
            at = lambda t, i, side: phi[t, rows_of(i), tile_at(j, (1 + side) * LANES)]
            force = [None] * slices
            for n in range(slices):
                t = n // 2 if n % 2 == 0 else slices - 1 - n // 2
                v = at(t, i, 0)
                before = low_ref[t : t + 1, lanes] if i == 0 else at(t, i - 1, 0)
                after = high_ref[t : t + 1, lanes] if i == blocks - 1 else at(t, i + 1, 0)
                total = neighbours(masks, v, before, after, at(t, i, -1), at(t, i, 1))
                force[t] = v * (table[LINEAR] + v * (table[SQUARE] + table[CUBE] * v)) - table[SCALE] * total
            forward, backward = [None] * slices, [None] * slices
            a, b = force[0], force[-1]
            backward[-1] = b
            r = table[DECAY]
            for t in range(1, slices):
                forward[t] = r * a
                a = force[t] + forward[t]
                s = slices - 1 - t
                b = force[s] + r * b
                backward[s] = b
            for t in range(slices):
                local = backward[t] if t == 0 else forward[t] + backward[t]
                value = table[KEEP] * at(t, i, 0) - local
                psi_ref[t, rows_of(i), place] = value
                if i == 0:
                    edges_ref[0, t : t + 1, place] = value[:1]
                if i == blocks - 1:
                    edges_ref[1, t : t + 1, place] = value[ROWS - 1 :]
        return carry

    lax.fori_loop(tiles[0], tiles[1], tile, 0, unroll=min(UNROLL, tiles[1] - tiles[0]))


def reads_of(tiles, count, source, target, offset, sems):
    width = source.shape[-1] // LANES
    bounds = [max(tiles[0] - 1, 0)]
    bounds += [tiles[0] + (tiles[1] - tiles[0]) * n // count + 1 for n in range(1, count)]
    bounds += [min(tiles[1] + 1, width)]
    reads = []
    for n, part in enumerate(zip(bounds, bounds[1:])):
        there = lanes_of(part[0] + offset, part[1] + offset)
        reads.append(pltpu.make_async_copy(source.at[:, :, lanes_of(*part)], target.at[:, :, there], sems.at[n]))
        reads[-1].start()
    return bounds, reads


def parts_of(tiles, count):
    bounds = [tiles[0] + (tiles[1] - tiles[0]) * n // count for n in range(count + 1)]
    return list(zip(bounds, bounds[1:]))


def first_relax_kernel(tiles, ready, table, low_ref, high_ref, old_ref, *rest):
    psi_ref, edges_ref, phi, stage, in_sems, out_sems = rest[-6:]
    count = in_sems.shape[0]
    _, reads = reads_of(tiles, count, old_ref, phi, 1, in_sems)
    clear_guards(phi)
    masks = Masks()
    writes = []
    for n, part in enumerate(parts_of(tiles, count)):
        reads[n].wait()
        relax_tiles(table, masks, phi, low_ref, high_ref, stage, edges_ref, part, tiles[0])
        here = lanes_of(part[0] - tiles[0], part[1] - tiles[0])
        writes.append(
            pltpu.make_async_copy(stage.at[:, :, here], psi_ref.at[:, :, lanes_of(*part)], out_sems.at[n])
        )
        writes[-1].start()
    for write in writes:
        write.wait()


def next_relax_kernel(
    tiles, ready, half_ref, table, own_ref, other_ref, low_ref, high_ref, old_ref, psi_ref, edges_ref, phi, old, sems
):
    slices, planes, _ = phi.shape
    blocks = planes // ROWS
    count = sems.shape[0]
    bounds, reads = reads_of(tiles, count, old_ref, old, 0, sems)
    clear_guards(phi)

    def tile(j, carry):
        lanes, inner = tile_at(j), tile_at(j, LANES)
        for i in range(blocks):
            both = entering_tile(table, half_ref, own_ref, other_ref, i, blocks, lanes)
            for k in range(slices // 2):
                v, w = entered_pair(table, both, old, k, i, lanes)
                phi[k, rows_of(i), inner] = v
                phi[slices - 1 - k, rows_of(i), inner] = w
        return carry

    masks = Masks()
    for n, part in enumerate(parts_of(tiles, count)):
        reads[n].wait()
        lax.fori_loop(bounds[n], bounds[n + 1], tile, 0, unroll=True)
        relax_tiles(table, masks, phi, low_ref, high_ref, psi_ref, edges_ref, part, tiles[0])


def last_kernel(half_ref, table, own_ref, other_ref, *rest):
    *olds, out_ref, stage, sems = rest
    slices, planes, width = stage.shape
    blocks = planes // ROWS
    writes = []
    for n, ((first, last), old) in enumerate(zip(pieces_of(width), olds)):
        middle = (first + last) // 2

        def tile(j, carry):
            lanes = tile_at(j)
            for i in range(blocks):
                both = entering_tile(table, half_ref, own_ref, other_ref, i, blocks, lanes)
                for k in range(slices // 2):
                    v, w = entered_pair(table, both, old, k, i, tile_at(j, -first * LANES))
                    stage[k, rows_of(i), lanes] = v
                    stage[slices - 1 - k, rows_of(i), lanes] = w
            return carry

        for k, part in enumerate(((first, middle), (middle, last))):
            lax.fori_loop(*part, tile, 0, unroll=True)
            lanes = lanes_of(*part)
            writes.append(pltpu.make_async_copy(stage.at[:, :, lanes], out_ref.at[:, :, lanes], sems.at[2 * n + k]))
            writes[-1].start()
    for write in writes:
        write.wait()


VMEM = pl.BlockSpec(memory_space=pltpu.VMEM)
SMEM = pl.BlockSpec(memory_space=pltpu.SMEM)
HBM = pl.BlockSpec(memory_space=pltpu.HBM)
PARAMS = pltpu.CompilerParams(vmem_limit_bytes=24 * 2**20)


def in_hbm(array):
    return pltpu.with_memory_space_constraint(array, pltpu.HBM)


def hbm(shape):
    return pltpu.HBM(shape, jnp.float32)


def f32(shape):
    return jax.ShapeDtypeStruct(shape, jnp.float32)


def padded(lead, shape):
    return pltpu.VMEM((lead, shape[1], shape[2] + 2 * LANES), jnp.float32)


def cost(shape, flops):
    size = shape[0] * shape[1] * shape[2]
    return pl.CostEstimate(flops=flops * size, bytes_accessed=4 * size, transcendentals=0)


def vmem(shape):
    return pltpu.VMEM(shape, jnp.float32)


def in_vmem(array):
    return pltpu.with_memory_space_constraint(array, pltpu.VMEM)


def piece_shape(shape, piece):
    return shape[0], shape[1], (piece[1] - piece[0]) * LANES


def first_sums(step, mass, field, levels):
    slices, planes, width = field.shape
    assert slices % 2 == 0 and levels < ROWS
    return pl.pallas_call(
        functools.partial(first_sums_kernel, levels),
        in_specs=[SMEM] * 2 + [HBM],
        out_shape=(
            f32((2, planes, width)),
            f32((WEIGHTS + slices, *TILE)),
            f32((4, slices, width)),
            f32((ROWS, width)),
        ),
        out_specs=(VMEM,) * 4,
        scratch_shapes=[
            pltpu.VMEM(field.shape, jnp.float32),
            padded(2, field.shape),
            pltpu.SemaphoreType.DMA((4,)),
        ],
        compiler_params=PARAMS,
        cost_estimate=cost(field.shape, 12),
    )(step, mass, in_hbm(field))


def next_sums(half, table, own, other, old):
    _, planes, width = old.shape
    return pl.pallas_call(
        next_sums_kernel,
        in_specs=[SMEM] + [VMEM] * 3 + [HBM],
        out_shape=f32((2, planes, width)),
        out_specs=VMEM,
        scratch_shapes=[
            pltpu.VMEM(old.shape, jnp.float32),
            padded(2, old.shape),
            pltpu.SemaphoreType.DMA((4,)),
        ],
        compiler_params=PARAMS,
        cost_estimate=cost(old.shape, 16),
    )(half, table, own, other, in_hbm(old))


def first_relax(tiles, ready, table, low, high, old, psi):
    slices, planes, width = old.shape
    piece = piece_shape(old.shape, tiles)
    operands = [ready, table, low, high, in_hbm(old)] + ([] if psi is None else [in_hbm(psi)])
    semaphores = pltpu.SemaphoreType.DMA((PARTS,))
    return pl.pallas_call(
        functools.partial(first_relax_kernel, tiles),
        in_specs=[VMEM] * 4 + [HBM] * (len(operands) - 4),
        out_shape=(hbm(old.shape), f32((2, slices, piece[-1]))),
        out_specs=(HBM, VMEM),
        input_output_aliases={} if psi is None else {5: 0},
        scratch_shapes=[padded(slices, old.shape), pltpu.VMEM(piece, jnp.float32), semaphores, semaphores],
        compiler_params=PARAMS,
        cost_estimate=cost(piece, 40),
    )(*operands)


def next_relax(tiles, ready, half, own, other, table, low, high, old):
    slices, planes, width = old.shape
    piece = piece_shape(old.shape, tiles)
    return pl.pallas_call(
        functools.partial(next_relax_kernel, tiles),
        in_specs=[VMEM, SMEM] + [VMEM] * 5 + [HBM],
        out_shape=(vmem(piece), f32((2, slices, piece[-1]))),
        out_specs=(VMEM, VMEM),
        scratch_shapes=[
            padded(slices, old.shape),
            pltpu.VMEM(old.shape, jnp.float32),
            pltpu.SemaphoreType.DMA((PARTS,)),
        ],
        compiler_params=PARAMS,
        cost_estimate=cost(piece, 40),
    )(ready, half, table, own, other, low, high, in_hbm(old))


def last_step(shape, half, table, own, other, olds):
    return pl.pallas_call(
        last_kernel,
        in_specs=[SMEM] + [VMEM] * (3 + len(olds)),
        out_shape=hbm(shape),
        out_specs=HBM,
        scratch_shapes=[pltpu.VMEM(shape, jnp.float32), pltpu.SemaphoreType.DMA((2 * len(olds),))],
        compiler_params=PARAMS,
        cost_estimate=cost(shape, 6),
    )(half, table, own, other, *map(in_vmem, olds))


class Loop:
    def __init__(self):
        self.devices = lax.axis_size("tm")
        self.me = lax.axis_index("tm")
        self.levels = self.devices.bit_length() - 1
        assert self.devices == 1 << self.levels and self.levels > 3

    def swap(self, array, offset):
        return lax.ppermute(array, "tm", [(i, i ^ offset) for i in range(self.devices)])

    def rho(self, level):
        return self.arcs[level : level + 1]

    def is_left(self, level):
        return (self.me >> level) & 1 == 0

    def merge(self, mine, theirs, level):
        left, rho = self.is_left(level), self.rho(level)
        ours, others = jnp.where(left, rho, 1.0), jnp.where(left, 1.0, rho)
        return jnp.stack([ours * mine[0] + others * theirs[0], others * mine[1] + ours * theirs[1]])

    def down(self, mine, theirs, both, level):
        left, rho = self.is_left(level), self.rho(level)
        before = jnp.where(left, both[0], theirs[0] + rho * both[0])
        after = jnp.where(left, theirs[1] + rho * both[1], both[1])
        return jnp.stack([before, after])

    def down_other(self, mine, theirs, both, level):
        left, rho = self.is_left(level), self.rho(level)
        before = jnp.where(left, mine[0] + rho * both[0], both[0])
        after = jnp.where(left, both[1], mine[1] + rho * both[1])
        return jnp.stack([before, after])

    def solve(self, ends, arcs, works):
        self.arcs = arcs
        half = ends.shape[1] // 2
        bit = self.me & 1
        mine0 = lax.dynamic_slice_in_dim(ends, bit * half, half, 1)
        theirs0 = self.swap(lax.dynamic_slice_in_dim(ends, (1 - bit) * half, half, 1), 1)
        chip = self.merge(mine0, theirs0, 0)

        group = (self.me >> 1) & 3
        quarter = half // 4

        def part(k):
            return lax.dynamic_slice_in_dim(chip, (group ^ k) * quarter, quarter, 1)

        a0 = part(0)
        received = [self.swap(part(k), 2 * k) for k in (1, 2, 3)]
        state = works[0](chip)
        (a1, a2, a3), state = lax.optimization_barrier((received, state))
        near, far = self.merge(a0, a1, 1), self.merge(a2, a3, 1)
        arc = self.merge(near, far, 2)
        stack = []
        for level in range(3, self.levels):
            theirs = self.swap(arc, 1 << level)
            if level == 3:
                state = works[1](arc, state)
                theirs, state = lax.optimization_barrier((theirs, state))
            stack.append((arc, theirs, level))
            arc = self.merge(arc, theirs, level)
        enters = arc * self.rho(self.levels)
        for mine, theirs, level in reversed(stack):
            enters = self.down(mine, theirs, enters, level)
        enters_near = self.down(near, far, enters, 2)
        enters_far = self.down_other(near, far, enters, 2)
        p0 = self.down(a0, a1, enters_near, 1)
        p1 = self.down_other(a0, a1, enters_near, 1)
        p2 = self.down(a2, a3, enters_far, 1)
        p3 = self.down_other(a2, a3, enters_far, 1)
        received = [self.swap(p, 2 * k) for k, p in ((1, p1), (2, p2), (3, p3))]
        state = works[2](enters, state)
        received, state = lax.optimization_barrier((received, state))
        back = jnp.stack([p0] + received)
        chip_enters = jnp.concatenate(
            [lax.dynamic_index_in_dim(back, group ^ k, 0, keepdims=False) for k in range(4)], axis=1
        )
        own = self.down(mine0, theirs0, chip_enters, 0)
        other = self.swap(self.down_other(mine0, theirs0, chip_enters, 0), 1)
        return own, other, state


class Planes:
    def __init__(self, planes):
        self.planes = planes
        self.devices = lax.axis_size("space")
        self.me = lax.axis_index("space")
        self.rounds = [p for p in (0, 1) if p + 1 < self.devices]

    def row(self, parity):
        return jnp.where(self.me % 2 == parity, self.planes - 1, 0)

    def exchange(self, first, last):
        low = high = jnp.zeros_like(first)
        for parity in self.rounds:
            given = jnp.where(self.row(parity) == 0, first, last)
            pairs = range(parity, self.devices - 1, 2)
            got = lax.ppermute(given, "space", [(i, i + 1) for i in pairs] + [(i + 1, i) for i in pairs])
            low = low + jnp.where(self.row(parity) == 0, got, 0.0)
            high = high + jnp.where(self.row(parity) == 0, 0.0, got)
        return low, high


def on_device(field, step, mass):
    shape = _, planes, width = field.shape
    loop = Loop()
    sides = Planes(planes)
    half = (loop.me & 1).astype(jnp.int32).reshape(1)

    pieces = pieces_of(width)

    def edge_sums(ends, low, high):
        row = lax.broadcasted_iota(jnp.int32, (1, planes, 1), 1)
        for place, plane in ((0, low), (planes - 1, high)):
            sums = jnp.sum(weights[2:] * plane[None], axis=1)
            ends = ends - jnp.where(row == place, sums[:, None, :], 0.0)
        return ends

    low, high = sides.exchange(field[:, 0], field[:, -1])
    ends, table, weights, arcs = first_sums(step, mass, field, loop.levels)

    def first_work(tiles, ready, state=(None, ())):
        psi, edge = first_relax(tiles, ready, table, low, high, field, state[0])
        return psi, (*state[1], edge)

    works = [functools.partial(first_work, tiles) for tiles in pieces]
    own, other, (psi, edges) = loop.solve(edge_sums(ends, low, high), arcs, works)

    edges = jnp.concatenate(edges, axis=2)
    mine = half[0] == 0
    fluxes = jnp.where(mine, own[:, 0], other[:, 0]), jnp.where(mine, other[:, -1], own[:, -1])
    low, high = sides.exchange(
        *(edge - weights[0] * flux[0] - weights[1] * flux[1] for edge, flux in zip(edges, fluxes))
    )
    ends = next_sums(half, table, own, other, psi)

    def next_work(tiles, ready, state=(), own=own, other=other):
        return *state, next_relax(tiles, ready, half, own, other, table, low, high, psi)[0]

    works = [functools.partial(next_work, tiles) for tiles in pieces]
    own, other, olds = loop.solve(edge_sums(ends, low, high), arcs, works)
    return last_step(shape, half, table, own, other, olds)


def solution(mesh):
    return jax.shard_map(
        on_device,
        mesh=mesh,
        in_specs=(P("tm", "space", None), P(), P()),
        out_specs=P("tm", "space", None),
        check_vma=False,
    )
```

```python
import functools

import jax
import jax.numpy as jnp
from jax import lax
from jax.experimental import pallas as pl
from jax.experimental.pallas import tpu as pltpu
from jax.sharding import PartitionSpec as P

NZ = 32

LANES = 128
ROWS = 8
TILE = (ROWS, LANES)
UNROLL = 4
PARTS = 3
READS = 8

DECAY, SCALE, LINEAR, SQUARE, CUBE, KEEP, WEIGHTS = range(7)


def decay(mass):
    root = jnp.sqrt(1.0 + 0.25 * mass * mass)
    return 1.0 + 0.5 * mass * mass - mass * root, 0.5 / (mass * root)


def fill_table(scalars, table, slices):
    step, mass = jnp.full(TILE, scalars[0], jnp.float32), jnp.full(TILE, scalars[1], jnp.float32)
    r, amplitude = decay(mass)
    scale = step * amplitude
    table[DECAY], table[SCALE], table[KEEP] = r, scale, 1.0 - step
    table[LINEAR], table[SQUARE], table[CUBE] = scale * (7.0 - mass * mass), -0.9 * scale, 0.25 * scale
    powers = [jnp.ones(TILE, jnp.float32)]
    for _ in range(slices - 1):
        powers.append(powers[-1] * r)
    for k in range(slices // 2):
        table[WEIGHTS + 2 * k] = 0.5 * (powers[k] + powers[slices - 1 - k])
        table[WEIGHTS + 2 * k + 1] = 0.5 * (powers[k] - powers[slices - 1 - k])


def fill_wide(scalars, planes_ref, arcs_ref, green_ref, levels):
    _, slices, width = planes_ref.shape

    def rate_of(shape):
        half = 0.5 * jnp.full(shape, scalars[1], jnp.float32)
        return 2.0 * jnp.log1p(half + half * half / (1.0 + jnp.sqrt(1.0 + half * half)))

    shape = (slices, LANES)
    rate = rate_of(shape)
    t = lax.broadcasted_iota(jnp.int32, shape, 0).astype(jnp.float32)
    mass = jnp.full(shape, scalars[1], jnp.float32)
    scale = jnp.full(shape, scalars[0], jnp.float32) * decay(mass)[1]
    start, end = jnp.exp(-rate * t), jnp.exp(-rate * (slices - 1 - t))
    r = jnp.exp(-rate)
    values = (r * start, r * end, scale * end, scale * start)
    green_ref[...] = scale * jnp.exp(-rate * jnp.abs(t - lax.broadcasted_iota(jnp.int32, shape, 1).astype(jnp.float32)))
    row = lax.broadcasted_iota(jnp.int32, TILE, 0)
    rate = rate_of(TILE)
    arcs = jnp.zeros(TILE, jnp.float32)
    for level in range(levels):
        arcs = jnp.where(row == level, jnp.exp(-rate * (slices << level)), arcs)
    arcs = jnp.where(row == levels, 1.0 / (1.0 - jnp.exp(-rate * (slices << levels))), arcs)

    def tile(j, carry):
        for n, value in enumerate(values):
            planes_ref[n, :, tile_at(j)] = value
        arcs_ref[:, tile_at(j)] = arcs
        return carry

    lax.fori_loop(0, width // LANES, tile, 0)


def rows_of(i):
    return slice(ROWS * i, ROWS * (i + 1))


def tile_at(j, offset=0):
    return pl.ds(pl.multiple_of(j * LANES + offset, LANES), LANES)


class Masks:
    def __init__(self):
        lane = lax.broadcasted_iota(jnp.int32, TILE, 1)
        row = lax.broadcasted_iota(jnp.int32, TILE, 0)
        self.first_z, self.last_z = lane % NZ == 0, lane % NZ == NZ - 1
        self.first_row, self.last_row = row == 0, row == ROWS - 1
        self.head, self.tail = lane < NZ, lane >= LANES - NZ


def neighbours(masks, v, before, after, left, right):
    total = pltpu.roll(jnp.where(masks.last_row, before, v), 1, 0)
    total = total + pltpu.roll(jnp.where(masks.first_row, after, v), ROWS - 1, 0)
    total = total + jnp.where(masks.first_z, 0.0, pltpu.roll(v, 1, 1))
    total = total + jnp.where(masks.last_z, 0.0, pltpu.roll(v, LANES - 1, 1))
    total = total + pltpu.roll(jnp.where(masks.tail, left, v), NZ, 1)
    return total + pltpu.roll(jnp.where(masks.head, right, v), LANES - NZ, 1)


def entering_tile(table, half_ref, own_ref, other_ref, i, blocks, lanes):
    half = 2 * i // blocks
    place = rows_of(i - half * blocks // 2)
    mine = half_ref[0] == half
    p = jnp.where(mine, own_ref[0, place, lanes], other_ref[0, place, lanes])
    q = jnp.where(mine, own_ref[1, place, lanes], other_ref[1, place, lanes])
    r = table[DECAY]
    return r * (p + q), r * (p - q)


def entered_pair(table, both, old, k, i, place):
    v, w = old[k, rows_of(i), place], old[old.shape[0] - 1 - k, rows_of(i), place]
    if both is None:
        return v, w
    even, odd = table[WEIGHTS + 2 * k] * both[0], table[WEIGHTS + 2 * k + 1] * both[1]
    return v - (even + odd), w - (even - odd)


def sum_tiles(table, enter, old, ends_ref, sums, tiles):
    slices, planes, _ = old.shape
    blocks = planes // ROWS

    def tile(j, carry):
        lanes = tile_at(j)
        for i in range(blocks):
            both = enter(i, lanes) if enter else None
            for k in range(slices // 2):
                v, w = entered_pair(table, both, old, k, i, lanes)
                f = v * v * (table[SQUARE] + table[CUBE] * v)
                g = w * w * (table[SQUARE] + table[CUBE] * w)
                a, b = table[WEIGHTS + 2 * k], table[WEIGHTS + 2 * k + 1]
                terms = (a * (v + w), b * (v - w), a * (f + g), b * (f - g))
                total = terms if k == 0 else tuple(x + y for x, y in zip(total, terms))
            for n, (field, force) in enumerate(
                ((total[0] - total[1], total[2] - total[3]), (total[0] + total[1], total[2] + total[3]))
            ):
                sums[n, rows_of(i), tile_at(j, LANES)] = field
                ends_ref[n, rows_of(i), lanes] = force + table[LINEAR] * field
        return carry

    lax.fori_loop(tiles[0], tiles[1], tile, 0, unroll=True)


def finish_sums(table, masks, ends_ref, sums, tiles):
    blocks = ends_ref.shape[1] // ROWS
    zero = jnp.zeros(TILE, jnp.float32)

    def tile(j, carry):
        for n in range(2):
            at = lambda i, side: sums[n, rows_of(i), tile_at(j, (1 + side) * LANES)]
            for i in range(blocks):
                before = zero if i == 0 else at(i - 1, 0)
                after = zero if i == blocks - 1 else at(i + 1, 0)
                total = neighbours(masks, at(i, 0), before, after, at(i, -1), at(i, 1))
                ends_ref[n, rows_of(i), tile_at(j)] -= table[SCALE] * total
        return carry

    lax.fori_loop(*tiles, tile, 0, unroll=True)


def clear_guards(ref):
    lead, planes, width = ref.shape
    guard = jnp.zeros((lead, planes, LANES), jnp.float32)
    ref[:, :, :LANES] = guard
    ref[:, :, width - LANES :] = guard


def bounds_of(width):
    tiles = width // LANES
    return [0, 7 * tiles // 16, 11 * tiles // 16, tiles]


def pieces_of(width):
    bounds = bounds_of(width)
    return list(zip(bounds, bounds[1:]))


def lanes_of(first, last):
    return slice(first * LANES, last * LANES)


def sum_parts(table, enter, source, ends_ref, old, sums, sems, prepare):
    tiles = ends_ref.shape[-1] // LANES
    count = sems.shape[0]
    reads = []
    for n in range(count):
        part = n * tiles // count, (n + 1) * tiles // count
        lanes = lanes_of(*part)
        reads.append((part, pltpu.make_async_copy(source.at[:, :, lanes], old.at[:, :, lanes], sems.at[n])))
        reads[-1][1].start()
    clear_guards(sums)
    prepare()
    masks = Masks()
    for part, read in reads:
        read.wait()
        sum_tiles(table, enter, old, ends_ref, sums, part)
        last = part[1] == tiles
        finish_sums(table, masks, ends_ref, sums, (max(part[0] - 1, 0), part[1] if last else part[1] - 1))


def first_sums_kernel(
    levels, step_ref, mass_ref, old_ref, ends_ref, table, planes_ref, arcs_ref, green_ref, old, sums, sems
):
    def prepare():
        values = step_ref[0], mass_ref[0]
        fill_table(values, table, old.shape[0])
        fill_wide(values, planes_ref, arcs_ref, green_ref, levels)

    sum_parts(table, None, old_ref, ends_ref, old, sums, sems, prepare)


def next_sums_kernel(half_ref, table, own_ref, other_ref, old_ref, ends_ref, old, sums, sems):
    blocks = ends_ref.shape[1] // ROWS

    def enter(i, lanes):
        return entering_tile(table, half_ref, own_ref, other_ref, i, blocks, lanes)

    sum_parts(table, enter, old_ref, ends_ref, old, sums, sems, lambda: None)


def relax_tiles(table, masks, phi, low_ref, high_ref, psi_ref, edges_ref, tiles, start):
    slices, planes, _ = phi.shape
    blocks = planes // ROWS
    zero = jnp.zeros(TILE, jnp.float32)

    def tile(j, carry):
        lanes, place = tile_at(j), tile_at(j, -start * LANES)
        for i in range(blocks):
            at = lambda t, i, side: phi[t, rows_of(i), tile_at(j, (1 + side) * LANES)]
            force = [None] * slices
            for n in range(slices):
                t = n // 2 if n % 2 == 0 else slices - 1 - n // 2
                v = at(t, i, 0)
                before = (zero if low_ref is None else low_ref[t : t + 1, lanes]) if i == 0 else at(t, i - 1, 0)
                after = (zero if high_ref is None else high_ref[t : t + 1, lanes]) if i == blocks - 1 else at(t, i + 1, 0)
                total = neighbours(masks, v, before, after, at(t, i, -1), at(t, i, 1))
                force[t] = v * (table[LINEAR] + v * (table[SQUARE] + table[CUBE] * v)) - table[SCALE] * total
            forward, backward = [None] * slices, [None] * slices
            a, b = force[0], force[-1]
            backward[-1] = b
            r = table[DECAY]
            for t in range(1, slices):
                forward[t] = r * a
                a = force[t] + forward[t]
                s = slices - 1 - t
                b = force[s] + r * b
                backward[s] = b
            for t in range(slices):
                local = backward[t] if t == 0 else forward[t] + backward[t]
                value = table[KEEP] * at(t, i, 0) - local
                psi_ref[t, rows_of(i), place] = value
                if edges_ref is not None and i == 0:
                    edges_ref[0, t : t + 1, place] = value[:1]
                if edges_ref is not None and i == blocks - 1:
                    edges_ref[1, t : t + 1, place] = value[ROWS - 1 :]
        return carry

    lax.fori_loop(tiles[0], tiles[1], tile, 0, unroll=min(UNROLL, tiles[1] - tiles[0]))


def reads_of(tiles, count, source, target, offset, sems):
    width = source.shape[-1] // LANES
    bounds = [max(tiles[0] - 1, 0)]
    bounds += [tiles[0] + (tiles[1] - tiles[0]) * n // count + 1 for n in range(1, count)]
    bounds += [min(tiles[1] + 1, width)]
    reads = []
    for n, part in enumerate(zip(bounds, bounds[1:])):
        there = lanes_of(part[0] + offset, part[1] + offset)
        reads.append(pltpu.make_async_copy(source.at[:, :, lanes_of(*part)], target.at[:, :, there], sems.at[n]))
        reads[-1].start()
    return bounds, reads


def parts_of(tiles, count):
    bounds = [tiles[0] + (tiles[1] - tiles[0]) * n // count for n in range(count + 1)]
    return list(zip(bounds, bounds[1:]))


def first_relax_kernel(tiles, ready, table, low_ref, high_ref, old_ref, *rest):
    psi_ref, edges_ref, phi, stage, in_sems, out_sems = rest[-6:]
    count = in_sems.shape[0]
    _, reads = reads_of(tiles, count, old_ref, phi, 1, in_sems)
    clear_guards(phi)
    masks = Masks()
    writes = []
    for n, part in enumerate(parts_of(tiles, count)):
        reads[n].wait()
        relax_tiles(table, masks, phi, low_ref, high_ref, stage, edges_ref, part, tiles[0])
        here = lanes_of(part[0] - tiles[0], part[1] - tiles[0])
        writes.append(
            pltpu.make_async_copy(stage.at[:, :, here], psi_ref.at[:, :, lanes_of(*part)], out_sems.at[n])
        )
        writes[-1].start()
    for write in writes:
        write.wait()


def next_relax_kernel(
    tiles, ready, half_ref, table, own_ref, other_ref, old_ref, psi_ref, phi, old, sems
):
    slices, planes, _ = phi.shape
    blocks = planes // ROWS
    count = sems.shape[0]
    bounds, reads = reads_of(tiles, count, old_ref, old, 0, sems)
    clear_guards(phi)

    def tile(j, carry):
        lanes, inner = tile_at(j), tile_at(j, LANES)
        for i in range(blocks):
            both = entering_tile(table, half_ref, own_ref, other_ref, i, blocks, lanes)
            for k in range(slices // 2):
                v, w = entered_pair(table, both, old, k, i, lanes)
                phi[k, rows_of(i), inner] = v
                phi[slices - 1 - k, rows_of(i), inner] = w
        return carry

    masks = Masks()
    for n, part in enumerate(parts_of(tiles, count)):
        reads[n].wait()
        lax.fori_loop(bounds[n], bounds[n + 1], tile, 0, unroll=True)
        relax_tiles(table, masks, phi, None, None, psi_ref, None, part, tiles[0])


def last_kernel(mine, pieces, half_ref, table, low_ref, high_ref, enters_ref, *rest):
    olds, (out_ref, stage, sems) = rest[: len(pieces)], rest[-3:]
    slices, planes, _ = stage.shape
    blocks = planes // ROWS
    base = half_ref[0] * planes if mine else (1 - half_ref[0]) * planes
    r = table[DECAY]
    row = lax.broadcasted_iota(jnp.int32, TILE, 0) + base
    writes = []
    for n, ((first, last), old) in enumerate(zip(pieces, olds)):

        def tile(j, carry):
            lanes, place = tile_at(j), tile_at(j, -first * LANES)

            def edge(t, i):
                value = 0.0
                if i == 0:
                    value += jnp.where(row == 0, low_ref[t : t + 1, lanes], 0.0)
                if i == blocks - 1:
                    value += jnp.where(row + ROWS * i == 2 * planes - 1, high_ref[t : t + 1, lanes], 0.0)
                return value

            for i in range(blocks):
                rows = pl.ds(pl.multiple_of(base + ROWS * i, ROWS), ROWS)
                p, q = enters_ref[0, rows_of(i), lanes], enters_ref[1, rows_of(i), lanes]
                even, odd = r * (p + q), r * (p - q)
                for k in range(slices // 2):
                    x, y = table[WEIGHTS + 2 * k] * even, table[WEIGHTS + 2 * k + 1] * odd
                    stage[k, rows_of(i), lanes] = old[k, rows, place] - (x + y) + edge(k, i)
                    t = slices - 1 - k
                    stage[t, rows_of(i), lanes] = old[t, rows, place] - (x - y) + edge(t, i)
            return carry

        lax.fori_loop(first, last, tile, 0, unroll=UNROLL)
        lanes = lanes_of(first, last)
        there = out_ref.at[:, pl.ds(pl.multiple_of(base, ROWS), planes), lanes]
        writes.append(pltpu.make_async_copy(stage.at[:, :, lanes], there, sems.at[n]))
        writes[-1].start()
    for write in writes:
        write.wait()


VMEM = pl.BlockSpec(memory_space=pltpu.VMEM)
SMEM = pl.BlockSpec(memory_space=pltpu.SMEM)
HBM = pl.BlockSpec(memory_space=pltpu.HBM)
PARAMS = pltpu.CompilerParams(vmem_limit_bytes=24 * 2**20)


def in_hbm(array):
    return pltpu.with_memory_space_constraint(array, pltpu.HBM)


def hbm(shape):
    return pltpu.HBM(shape, jnp.float32)


def f32(shape):
    return jax.ShapeDtypeStruct(shape, jnp.float32)


def padded(lead, shape):
    return pltpu.VMEM((lead, shape[1], shape[2] + 2 * LANES), jnp.float32)


def cost(shape, flops):
    size = shape[0] * shape[1] * shape[2]
    return pl.CostEstimate(flops=flops * size, bytes_accessed=4 * size, transcendentals=0)


def vmem(shape):
    return pltpu.VMEM(shape, jnp.float32)


def in_vmem(array):
    return pltpu.with_memory_space_constraint(array, pltpu.VMEM)


def piece_shape(shape, piece):
    return shape[0], shape[1], (piece[1] - piece[0]) * LANES


def first_sums(step, mass, field, levels):
    slices, planes, width = field.shape
    assert slices % 2 == 0 and slices <= LANES and levels < ROWS
    return pl.pallas_call(
        functools.partial(first_sums_kernel, levels),
        in_specs=[SMEM] * 2 + [HBM],
        out_shape=(
            f32((2, planes, width)),
            f32((WEIGHTS + slices, *TILE)),
            f32((4, slices, width)),
            f32((ROWS, width)),
            f32((slices, LANES)),
        ),
        out_specs=(VMEM,) * 5,
        scratch_shapes=[
            pltpu.VMEM(field.shape, jnp.float32),
            padded(2, field.shape),
            pltpu.SemaphoreType.DMA((READS,)),
        ],
        compiler_params=PARAMS,
        cost_estimate=cost(field.shape, 12),
    )(step, mass, in_hbm(field))


def next_sums(half, table, own, other, old):
    _, planes, width = old.shape
    return pl.pallas_call(
        next_sums_kernel,
        in_specs=[SMEM] + [VMEM] * 3 + [HBM],
        out_shape=f32((2, planes, width)),
        out_specs=VMEM,
        scratch_shapes=[
            pltpu.VMEM(old.shape, jnp.float32),
            padded(2, old.shape),
            pltpu.SemaphoreType.DMA((READS,)),
        ],
        compiler_params=PARAMS,
        cost_estimate=cost(old.shape, 16),
    )(half, table, own, other, in_hbm(old))


def first_relax(tiles, ready, table, low, high, old, psi):
    slices, planes, width = old.shape
    piece = piece_shape(old.shape, tiles)
    operands = [ready, table, low, high, in_hbm(old)] + ([] if psi is None else [in_hbm(psi)])
    semaphores = pltpu.SemaphoreType.DMA((PARTS,))
    return pl.pallas_call(
        functools.partial(first_relax_kernel, tiles),
        in_specs=[VMEM] * 4 + [HBM] * (len(operands) - 4),
        out_shape=(hbm(old.shape), f32((2, slices, piece[-1]))),
        out_specs=(HBM, VMEM),
        input_output_aliases={} if psi is None else {5: 0},
        scratch_shapes=[padded(slices, old.shape), pltpu.VMEM(piece, jnp.float32), semaphores, semaphores],
        compiler_params=PARAMS,
        cost_estimate=cost(piece, 40),
    )(*operands)


def next_relax(tiles, ready, half, own, other, table, old):
    slices, planes, width = old.shape
    piece = piece_shape(old.shape, tiles)
    return pl.pallas_call(
        functools.partial(next_relax_kernel, tiles),
        in_specs=[VMEM, SMEM] + [VMEM] * 3 + [HBM],
        out_shape=vmem(piece),
        out_specs=VMEM,
        scratch_shapes=[
            padded(slices, old.shape),
            pltpu.VMEM(old.shape, jnp.float32),
            pltpu.SemaphoreType.DMA((PARTS,)),
        ],
        compiler_params=PARAMS,
        cost_estimate=cost(piece, 40),
    )(ready, half, table, own, other, in_hbm(old))


def last_step(shape, mine, half, table, low, high, enters, olds, out):
    slices, planes, width = shape
    pieces = pieces_of(width)
    operands = [half, table, low, high, enters, *map(in_vmem, olds)] + ([] if out is None else [in_hbm(out)])
    return pl.pallas_call(
        functools.partial(last_kernel, mine, pieces),
        in_specs=[SMEM] + [VMEM] * (4 + len(olds)) + ([] if out is None else [HBM]),
        out_shape=hbm(shape),
        out_specs=HBM,
        input_output_aliases={} if out is None else {len(operands) - 1: 0},
        scratch_shapes=[
            pltpu.VMEM((slices, planes // 2, width), jnp.float32),
            pltpu.SemaphoreType.DMA((len(pieces),)),
        ],
        compiler_params=PARAMS,
        cost_estimate=cost((slices, planes // 2, width), 6),
    )(*operands)


class Loop:
    def __init__(self):
        self.devices = lax.axis_size("tm")
        self.me = lax.axis_index("tm")
        self.levels = self.devices.bit_length() - 1
        assert self.devices == 1 << self.levels and self.levels > 3

    def swap(self, array, offset):
        return lax.ppermute(array, "tm", [(i, i ^ offset) for i in range(self.devices)])

    def rho(self, level):
        return self.arcs[level : level + 1]

    def is_left(self, level):
        return (self.me >> level) & 1 == 0

    def merge(self, mine, theirs, level):
        left, rho = self.is_left(level), self.rho(level)
        ours, others = jnp.where(left, rho, 1.0), jnp.where(left, 1.0, rho)
        return jnp.stack([ours * mine[0] + others * theirs[0], others * mine[1] + ours * theirs[1]])

    def down(self, mine, theirs, both, level):
        left, rho = self.is_left(level), self.rho(level)
        before = jnp.where(left, both[0], theirs[0] + rho * both[0])
        after = jnp.where(left, theirs[1] + rho * both[1], both[1])
        return jnp.stack([before, after])

    def down_other(self, mine, theirs, both, level):
        left, rho = self.is_left(level), self.rho(level)
        before = jnp.where(left, mine[0] + rho * both[0], both[0])
        after = jnp.where(left, both[1], mine[1] + rho * both[1])
        return jnp.stack([before, after])

    def solve(self, ends, arcs, works):
        self.arcs = arcs
        half = ends.shape[1] // 2
        bit = self.me & 1
        mine0 = lax.dynamic_slice_in_dim(ends, bit * half, half, 1)
        theirs0 = self.swap(lax.dynamic_slice_in_dim(ends, (1 - bit) * half, half, 1), 1)
        chip = self.merge(mine0, theirs0, 0)

        group = (self.me >> 1) & 3
        quarter = half // 4

        def part(k):
            return lax.dynamic_slice_in_dim(chip, (group ^ k) * quarter, quarter, 1)

        a0 = part(0)
        received = [self.swap(part(k), 2 * k) for k in (1, 2, 3)]
        state = works[0](chip)
        (a1, a2, a3), state = lax.optimization_barrier((received, state))
        near, far = self.merge(a0, a1, 1), self.merge(a2, a3, 1)
        arc = self.merge(near, far, 2)
        stack = []
        for level in range(3, self.levels):
            theirs = self.swap(arc, 1 << level)
            if level == 3:
                state = works[1](arc, state)
                theirs, state = lax.optimization_barrier((theirs, state))
            stack.append((arc, theirs, level))
            arc = self.merge(arc, theirs, level)
        enters = arc * self.rho(self.levels)
        for mine, theirs, level in reversed(stack):
            enters = self.down(mine, theirs, enters, level)
        enters_near = self.down(near, far, enters, 2)
        enters_far = self.down_other(near, far, enters, 2)
        p0 = self.down(a0, a1, enters_near, 1)
        p1 = self.down_other(a0, a1, enters_near, 1)
        p2 = self.down(a2, a3, enters_far, 1)
        p3 = self.down_other(a2, a3, enters_far, 1)
        received = [self.swap(p, 2 * k) for k, p in ((1, p1), (2, p2), (3, p3))]
        state = works[2](enters, state)
        received, state = lax.optimization_barrier((received, state))
        back = jnp.stack([p0] + received)
        chip_enters = jnp.concatenate(
            [lax.dynamic_index_in_dim(back, group ^ k, 0, keepdims=False) for k in range(4)], axis=1
        )
        own = self.down(mine0, theirs0, chip_enters, 0)
        other = self.swap(self.down_other(mine0, theirs0, chip_enters, 0), 1)
        return own, other, state


class Planes:
    def __init__(self, planes):
        self.planes = planes
        self.devices = lax.axis_size("space")
        self.me = lax.axis_index("space")
        self.rounds = [p for p in (0, 1) if p + 1 < self.devices]

    def row(self, parity):
        return jnp.where(self.me % 2 == parity, self.planes - 1, 0)

    def exchange(self, plane):
        low = high = 0.0
        for parity in self.rounds:
            row = self.row(parity)
            pairs = range(parity, self.devices - 1, 2)
            got = lax.ppermute(plane(row), "space", [(i, i + 1) for i in pairs] + [(i + 1, i) for i in pairs])
            low = low + jnp.where(row == 0, got, 0.0)
            high = high + jnp.where(row == 0, 0.0, got)
        return low, high


def on_device(field, step, mass):
    shape = _, planes, width = field.shape
    loop = Loop()
    sides = Planes(planes)
    half = (loop.me & 1).astype(jnp.int32).reshape(1)

    pieces = pieces_of(width)

    def sums_of(plane):
        return jnp.sum(weights[2:] * plane[None], axis=1)

    def with_edges(ends, first, last):
        row = lax.broadcasted_iota(jnp.int32, (1, planes, 1), 1)
        for place, sums in ((0, first), (planes - 1, last)):
            ends = ends - jnp.where(row == place, sums[:, None, :], 0.0)
        return ends

    low, high = sides.exchange(lambda row: lax.dynamic_index_in_dim(field, row, 1, keepdims=False))
    ends, table, weights, arcs, green = first_sums(step, mass, field, loop.levels)

    def first_work(tiles, ready, state=(None, ())):
        psi, edge = first_relax(tiles, ready, table, low, high, field, state[0])
        return psi, (*state[1], edge)

    works = [functools.partial(first_work, tiles) for tiles in pieces]
    own, other, (psi, edges) = loop.solve(with_edges(ends, sums_of(low), sums_of(high)), arcs, works)

    edges = jnp.concatenate(edges, axis=2)
    mine = half[0] == 0
    fluxes = jnp.where(mine, own[:, 0], other[:, 0]), jnp.where(mine, other[:, -1], own[:, -1])
    first, last = (edge - weights[0] * flux[0] - weights[1] * flux[1] for edge, flux in zip(edges, fluxes))
    halo = lambda row: jnp.where(row == 0, first, last)
    sums = sides.exchange(lambda row: sums_of(halo(row)))
    ends = with_edges(next_sums(half, table, own, other, psi), *sums)
    ends, first, last = lax.optimization_barrier((ends, first, last))
    low, high = sides.exchange(halo)

    def next_work(tiles, ready, state=(), own=own, other=other):
        return *state, next_relax(tiles, ready, half, own, other, table, psi)

    works = [functools.partial(next_work, tiles) for tiles in pieces]
    own, other, olds = loop.solve(ends, arcs, works)
    low, high = (jnp.dot(green[:, : field.shape[0]], plane, precision=lax.Precision.HIGHEST) for plane in (low, high))
    out = last_step(shape, True, half, table, low, high, own, olds, None)
    return last_step(shape, False, half, table, low, high, other, olds, out)


def solution(mesh):
    return jax.shard_map(
        on_device,
        mesh=mesh,
        in_specs=(P("tm", "space", None), P(), P()),
        out_specs=P("tm", "space", None),
        check_vma=False,
    )
```

```python
import functools

import jax
import jax.numpy as jnp
from jax import lax
from jax.experimental import pallas as pl
from jax.experimental.pallas import tpu as pltpu
from jax.sharding import PartitionSpec as P

NZ = 32

LANES = 128
ROWS = 8
TILE = (ROWS, LANES)
UNROLL = 4
PARTS = 3
READS = 8

DECAY, SCALE, LINEAR, SQUARE, CUBE, KEEP, WEIGHTS = range(7)


def decay(mass):
    root = jnp.sqrt(1.0 + 0.25 * mass * mass)
    return 1.0 + 0.5 * mass * mass - mass * root, 0.5 / (mass * root)


def fill_table(scalars, table, slices):
    step, mass = jnp.full(TILE, scalars[0], jnp.float32), jnp.full(TILE, scalars[1], jnp.float32)
    r, amplitude = decay(mass)
    scale = step * amplitude
    table[DECAY], table[SCALE], table[KEEP] = r, scale, 1.0 - step
    table[LINEAR], table[SQUARE], table[CUBE] = scale * (7.0 - mass * mass), -0.9 * scale, 0.25 * scale
    powers = [jnp.ones(TILE, jnp.float32)]
    for _ in range(slices - 1):
        powers.append(powers[-1] * r)
    for k in range(slices // 2):
        table[WEIGHTS + 2 * k] = 0.5 * (powers[k] + powers[slices - 1 - k])
        table[WEIGHTS + 2 * k + 1] = 0.5 * (powers[k] - powers[slices - 1 - k])


def fill_wide(scalars, planes_ref, arcs_ref, green_ref, levels):
    _, slices, width = planes_ref.shape

    def rate_of(shape):
        half = 0.5 * jnp.full(shape, scalars[1], jnp.float32)
        return 2.0 * jnp.log1p(half + half * half / (1.0 + jnp.sqrt(1.0 + half * half)))

    shape = (slices, LANES)
    rate = rate_of(shape)
    t = lax.broadcasted_iota(jnp.int32, shape, 0).astype(jnp.float32)
    mass = jnp.full(shape, scalars[1], jnp.float32)
    scale = jnp.full(shape, scalars[0], jnp.float32) * decay(mass)[1]
    start, end = jnp.exp(-rate * t), jnp.exp(-rate * (slices - 1 - t))
    r = jnp.exp(-rate)
    values = (r * start, r * end, scale * end, scale * start)
    green_ref[...] = scale * jnp.exp(-rate * jnp.abs(t - lax.broadcasted_iota(jnp.int32, shape, 1).astype(jnp.float32)))
    row = lax.broadcasted_iota(jnp.int32, TILE, 0)
    rate = rate_of(TILE)
    arcs = jnp.zeros(TILE, jnp.float32)
    for level in range(levels):
        arcs = jnp.where(row == level, jnp.exp(-rate * (slices << level)), arcs)
    arcs = jnp.where(row == levels, 1.0 / (1.0 - jnp.exp(-rate * (slices << levels))), arcs)

    def tile(j, carry):
        for n, value in enumerate(values):
            planes_ref[n, :, tile_at(j)] = value
        arcs_ref[:, tile_at(j)] = arcs
        return carry

    lax.fori_loop(0, width // LANES, tile, 0)


def rows_of(i):
    return slice(ROWS * i, ROWS * (i + 1))


def tile_at(j, offset=0):
    return pl.ds(pl.multiple_of(j * LANES + offset, LANES), LANES)


class Masks:
    def __init__(self):
        lane = lax.broadcasted_iota(jnp.int32, TILE, 1)
        row = lax.broadcasted_iota(jnp.int32, TILE, 0)
        self.first_z, self.last_z = lane % NZ == 0, lane % NZ == NZ - 1
        self.first_row, self.last_row = row == 0, row == ROWS - 1
        self.head, self.tail = lane < NZ, lane >= LANES - NZ


def neighbours(masks, v, before, after, left, right):
    total = pltpu.roll(jnp.where(masks.last_row, before, v), 1, 0)
    total = total + pltpu.roll(jnp.where(masks.first_row, after, v), ROWS - 1, 0)
    total = total + jnp.where(masks.first_z, 0.0, pltpu.roll(v, 1, 1))
    total = total + jnp.where(masks.last_z, 0.0, pltpu.roll(v, LANES - 1, 1))
    total = total + pltpu.roll(jnp.where(masks.tail, left, v), NZ, 1)
    return total + pltpu.roll(jnp.where(masks.head, right, v), LANES - NZ, 1)


def entering_tile(table, half_ref, own_ref, other_ref, i, blocks, lanes):
    half = 2 * i // blocks
    place = rows_of(i - half * blocks // 2)
    mine = half_ref[0] == half
    p = jnp.where(mine, own_ref[0, place, lanes], other_ref[0, place, lanes])
    q = jnp.where(mine, own_ref[1, place, lanes], other_ref[1, place, lanes])
    r = table[DECAY]
    return r * (p + q), r * (p - q)


def entered_pair(table, both, old, k, i, place):
    v, w = old[k, rows_of(i), place], old[old.shape[0] - 1 - k, rows_of(i), place]
    if both is None:
        return v, w
    even, odd = table[WEIGHTS + 2 * k] * both[0], table[WEIGHTS + 2 * k + 1] * both[1]
    return v - (even + odd), w - (even - odd)


def sum_tiles(table, enter, old, ends_ref, sums, tiles):
    slices, planes, _ = old.shape
    blocks = planes // ROWS

    def tile(j, carry):
        lanes = tile_at(j)
        for i in range(blocks):
            both = enter(i, lanes) if enter else None
            for k in range(slices // 2):
                v, w = entered_pair(table, both, old, k, i, lanes)
                f = v * v * (table[SQUARE] + table[CUBE] * v)
                g = w * w * (table[SQUARE] + table[CUBE] * w)
                a, b = table[WEIGHTS + 2 * k], table[WEIGHTS + 2 * k + 1]
                terms = (a * (v + w), b * (v - w), a * (f + g), b * (f - g))
                total = terms if k == 0 else tuple(x + y for x, y in zip(total, terms))
            for n, (field, force) in enumerate(
                ((total[0] - total[1], total[2] - total[3]), (total[0] + total[1], total[2] + total[3]))
            ):
                sums[n, rows_of(i), tile_at(j, LANES)] = field
                ends_ref[n, rows_of(i), lanes] = force + table[LINEAR] * field
        return carry

    lax.fori_loop(tiles[0], tiles[1], tile, 0, unroll=True)


def finish_sums(table, masks, ends_ref, sums, tiles):
    blocks = ends_ref.shape[1] // ROWS
    zero = jnp.zeros(TILE, jnp.float32)

    def tile(j, carry):
        for n in range(2):
            at = lambda i, side: sums[n, rows_of(i), tile_at(j, (1 + side) * LANES)]
            for i in range(blocks):
                before = zero if i == 0 else at(i - 1, 0)
                after = zero if i == blocks - 1 else at(i + 1, 0)
                total = neighbours(masks, at(i, 0), before, after, at(i, -1), at(i, 1))
                ends_ref[n, rows_of(i), tile_at(j)] -= table[SCALE] * total
        return carry

    lax.fori_loop(*tiles, tile, 0, unroll=True)


def clear_guards(ref):
    lead, planes, width = ref.shape
    guard = jnp.zeros((lead, planes, LANES), jnp.float32)
    ref[:, :, :LANES] = guard
    ref[:, :, width - LANES :] = guard


def bounds_of(width):
    tiles = width // LANES
    return [0, 7 * tiles // 16, 11 * tiles // 16, tiles]


def pieces_of(width):
    bounds = bounds_of(width)
    return list(zip(bounds, bounds[1:]))


def lanes_of(first, last):
    return slice(first * LANES, last * LANES)


def sum_parts(table, enter, source, ends_ref, old, sums, sems, prepare):
    tiles = ends_ref.shape[-1] // LANES
    count = sems.shape[0]
    reads = []
    for n in range(count):
        part = n * tiles // count, (n + 1) * tiles // count
        lanes = lanes_of(*part)
        reads.append((part, pltpu.make_async_copy(source.at[:, :, lanes], old.at[:, :, lanes], sems.at[n])))
        reads[-1][1].start()
    clear_guards(sums)
    prepare()
    masks = Masks()
    for part, read in reads:
        read.wait()
        sum_tiles(table, enter, old, ends_ref, sums, part)
        last = part[1] == tiles
        finish_sums(table, masks, ends_ref, sums, (max(part[0] - 1, 0), part[1] if last else part[1] - 1))


def first_sums_kernel(
    levels, step_ref, mass_ref, old_ref, ends_ref, table, planes_ref, arcs_ref, green_ref, old, sums, sems
):
    def prepare():
        values = step_ref[0], mass_ref[0]
        fill_table(values, table, old.shape[0])
        fill_wide(values, planes_ref, arcs_ref, green_ref, levels)

    sum_parts(table, None, old_ref, ends_ref, old, sums, sems, prepare)


def next_sums_kernel(half_ref, table, own_ref, other_ref, old_ref, ends_ref, old, sums, sems):
    blocks = ends_ref.shape[1] // ROWS

    def enter(i, lanes):
        return entering_tile(table, half_ref, own_ref, other_ref, i, blocks, lanes)

    sum_parts(table, enter, old_ref, ends_ref, old, sums, sems, lambda: None)


def relax_tiles(table, masks, phi, low_ref, high_ref, psi_ref, edges_ref, tiles, start):
    slices, planes, _ = phi.shape
    blocks = planes // ROWS
    zero = jnp.zeros(TILE, jnp.float32)

    def tile(j, carry):
        lanes, place = tile_at(j), tile_at(j, -start * LANES)
        for i in range(blocks):
            at = lambda t, i, side: phi[t, rows_of(i), tile_at(j, (1 + side) * LANES)]
            force = [None] * slices
            for n in range(slices):
                t = n // 2 if n % 2 == 0 else slices - 1 - n // 2
                v = at(t, i, 0)
                before = (zero if low_ref is None else low_ref[t : t + 1, lanes]) if i == 0 else at(t, i - 1, 0)
                after = (zero if high_ref is None else high_ref[t : t + 1, lanes]) if i == blocks - 1 else at(t, i + 1, 0)
                total = neighbours(masks, v, before, after, at(t, i, -1), at(t, i, 1))
                force[t] = v * (table[LINEAR] + v * (table[SQUARE] + table[CUBE] * v)) - table[SCALE] * total
            forward, backward = [None] * slices, [None] * slices
            a, b = force[0], force[-1]
            backward[-1] = b
            r = table[DECAY]
            for t in range(1, slices):
                forward[t] = r * a
                a = force[t] + forward[t]
                s = slices - 1 - t
                b = force[s] + r * b
                backward[s] = b
            for t in range(slices):
                local = backward[t] if t == 0 else forward[t] + backward[t]
                value = table[KEEP] * at(t, i, 0) - local
                psi_ref[t, rows_of(i), place] = value
                if edges_ref is not None and i == 0:
                    edges_ref[0, t : t + 1, place] = value[:1]
                if edges_ref is not None and i == blocks - 1:
                    edges_ref[1, t : t + 1, place] = value[ROWS - 1 :]
        return carry

    lax.fori_loop(tiles[0], tiles[1], tile, 0, unroll=min(UNROLL, tiles[1] - tiles[0]))


def reads_of(tiles, count, source, target, offset, sems):
    width = source.shape[-1] // LANES
    bounds = [max(tiles[0] - 1, 0)]
    bounds += [tiles[0] + (tiles[1] - tiles[0]) * n // count + 1 for n in range(1, count)]
    bounds += [min(tiles[1] + 1, width)]
    reads = []
    for n, part in enumerate(zip(bounds, bounds[1:])):
        there = lanes_of(part[0] + offset, part[1] + offset)
        reads.append(pltpu.make_async_copy(source.at[:, :, lanes_of(*part)], target.at[:, :, there], sems.at[n]))
        reads[-1].start()
    return bounds, reads


def parts_of(tiles, count):
    bounds = [tiles[0] + (tiles[1] - tiles[0]) * n // count for n in range(count + 1)]
    return list(zip(bounds, bounds[1:]))


def first_relax_kernel(tiles, ready, table, low_ref, high_ref, old_ref, *rest):
    psi_ref, edges_ref, phi, stage, in_sems, out_sems = rest[-6:]
    count = in_sems.shape[0]
    _, reads = reads_of(tiles, count, old_ref, phi, 1, in_sems)
    clear_guards(phi)
    masks = Masks()
    writes = []
    for n, part in enumerate(parts_of(tiles, count)):
        reads[n].wait()
        relax_tiles(table, masks, phi, low_ref, high_ref, stage, edges_ref, part, tiles[0])
        here = lanes_of(part[0] - tiles[0], part[1] - tiles[0])
        writes.append(
            pltpu.make_async_copy(stage.at[:, :, here], psi_ref.at[:, :, lanes_of(*part)], out_sems.at[n])
        )
        writes[-1].start()
    for write in writes:
        write.wait()


def next_relax_kernel(
    tiles, ready, half_ref, table, own_ref, other_ref, old_ref, psi_ref, phi, old, sems
):
    slices, planes, _ = phi.shape
    blocks = planes // ROWS
    count = sems.shape[0]
    bounds, reads = reads_of(tiles, count, old_ref, old, 0, sems)
    clear_guards(phi)

    def tile(j, carry):
        lanes, inner = tile_at(j), tile_at(j, LANES)
        for i in range(blocks):
            both = entering_tile(table, half_ref, own_ref, other_ref, i, blocks, lanes)
            for k in range(slices // 2):
                v, w = entered_pair(table, both, old, k, i, lanes)
                phi[k, rows_of(i), inner] = v
                phi[slices - 1 - k, rows_of(i), inner] = w
        return carry

    masks = Masks()
    for n, part in enumerate(parts_of(tiles, count)):
        reads[n].wait()
        lax.fori_loop(bounds[n], bounds[n + 1], tile, 0, unroll=True)
        relax_tiles(table, masks, phi, None, None, psi_ref, None, part, tiles[0])


def chunks_of(first, last):
    return [(a, min(a + 2, last)) for a in range(first, last, 2)]


def last_kernel(mine, pieces, half_ref, table, low_ref, high_ref, enters_ref, *rest):
    olds, (out_ref, stage, sems) = rest[: len(pieces)], rest[-3:]
    slices, planes, _ = stage.shape
    blocks = planes // ROWS
    base = half_ref[0] * planes if mine else (1 - half_ref[0]) * planes
    r = table[DECAY]
    row = lax.broadcasted_iota(jnp.int32, TILE, 0) + base
    writes = []
    for (first, last), old in zip(pieces, olds):

        def tile(j, carry):
            lanes, place = tile_at(j), tile_at(j, -first * LANES)

            def edge(t, i):
                value = 0.0
                if i == 0:
                    value += jnp.where(row == 0, low_ref[t : t + 1, lanes], 0.0)
                if i == blocks - 1:
                    value += jnp.where(row + ROWS * i == 2 * planes - 1, high_ref[t : t + 1, lanes], 0.0)
                return value

            for i in range(blocks):
                rows = pl.ds(pl.multiple_of(base + ROWS * i, ROWS), ROWS)
                p, q = enters_ref[0, rows_of(i), lanes], enters_ref[1, rows_of(i), lanes]
                even, odd = r * (p + q), r * (p - q)
                for k in range(slices // 2):
                    x, y = table[WEIGHTS + 2 * k] * even, table[WEIGHTS + 2 * k + 1] * odd
                    stage[k, rows_of(i), lanes] = old[k, rows, place] - (x + y) + edge(k, i)
                    t = slices - 1 - k
                    stage[t, rows_of(i), lanes] = old[t, rows, place] - (x - y) + edge(t, i)
            return carry

        for part in chunks_of(first, last):
            lax.fori_loop(*part, tile, 0, unroll=True)
            lanes = lanes_of(*part)
            there = out_ref.at[:, pl.ds(pl.multiple_of(base, ROWS), planes), lanes]
            writes.append(pltpu.make_async_copy(stage.at[:, :, lanes], there, sems.at[len(writes)]))
            writes[-1].start()
    for write in writes:
        write.wait()


VMEM = pl.BlockSpec(memory_space=pltpu.VMEM)
SMEM = pl.BlockSpec(memory_space=pltpu.SMEM)
HBM = pl.BlockSpec(memory_space=pltpu.HBM)
PARAMS = pltpu.CompilerParams(vmem_limit_bytes=24 * 2**20)


def in_hbm(array):
    return pltpu.with_memory_space_constraint(array, pltpu.HBM)


def hbm(shape):
    return pltpu.HBM(shape, jnp.float32)


def f32(shape):
    return jax.ShapeDtypeStruct(shape, jnp.float32)


def padded(lead, shape):
    return pltpu.VMEM((lead, shape[1], shape[2] + 2 * LANES), jnp.float32)


def cost(shape, flops):
    size = shape[0] * shape[1] * shape[2]
    return pl.CostEstimate(flops=flops * size, bytes_accessed=4 * size, transcendentals=0)


def vmem(shape):
    return pltpu.VMEM(shape, jnp.float32)


def in_vmem(array):
    return pltpu.with_memory_space_constraint(array, pltpu.VMEM)


def piece_shape(shape, piece):
    return shape[0], shape[1], (piece[1] - piece[0]) * LANES


def first_sums(step, mass, field, levels):
    slices, planes, width = field.shape
    assert slices % 2 == 0 and slices <= LANES and levels < ROWS
    return pl.pallas_call(
        functools.partial(first_sums_kernel, levels),
        in_specs=[SMEM] * 2 + [HBM],
        out_shape=(
            f32((2, planes, width)),
            f32((WEIGHTS + slices, *TILE)),
            f32((4, slices, width)),
            f32((ROWS, width)),
            f32((slices, LANES)),
        ),
        out_specs=(VMEM,) * 5,
        scratch_shapes=[
            pltpu.VMEM(field.shape, jnp.float32),
            padded(2, field.shape),
            pltpu.SemaphoreType.DMA((READS,)),
        ],
        compiler_params=PARAMS,
        cost_estimate=cost(field.shape, 12),
    )(step, mass, in_hbm(field))


def next_sums(half, table, own, other, old):
    _, planes, width = old.shape
    return pl.pallas_call(
        next_sums_kernel,
        in_specs=[SMEM] + [VMEM] * 3 + [HBM],
        out_shape=f32((2, planes, width)),
        out_specs=VMEM,
        scratch_shapes=[
            pltpu.VMEM(old.shape, jnp.float32),
            padded(2, old.shape),
            pltpu.SemaphoreType.DMA((READS,)),
        ],
        compiler_params=PARAMS,
        cost_estimate=cost(old.shape, 16),
    )(half, table, own, other, in_hbm(old))


def first_relax(tiles, ready, table, low, high, old, psi):
    slices, planes, width = old.shape
    piece = piece_shape(old.shape, tiles)
    operands = [ready, table, low, high, in_hbm(old)] + ([] if psi is None else [in_hbm(psi)])
    semaphores = pltpu.SemaphoreType.DMA((PARTS,))
    return pl.pallas_call(
        functools.partial(first_relax_kernel, tiles),
        in_specs=[VMEM] * 4 + [HBM] * (len(operands) - 4),
        out_shape=(hbm(old.shape), f32((2, slices, piece[-1]))),
        out_specs=(HBM, VMEM),
        input_output_aliases={} if psi is None else {5: 0},
        scratch_shapes=[padded(slices, old.shape), pltpu.VMEM(piece, jnp.float32), semaphores, semaphores],
        compiler_params=PARAMS,
        cost_estimate=cost(piece, 40),
    )(*operands)


def next_relax(tiles, ready, half, own, other, table, old):
    slices, planes, width = old.shape
    piece = piece_shape(old.shape, tiles)
    return pl.pallas_call(
        functools.partial(next_relax_kernel, tiles),
        in_specs=[VMEM, SMEM] + [VMEM] * 3 + [HBM],
        out_shape=vmem(piece),
        out_specs=VMEM,
        scratch_shapes=[
            padded(slices, old.shape),
            pltpu.VMEM(old.shape, jnp.float32),
            pltpu.SemaphoreType.DMA((PARTS,)),
        ],
        compiler_params=PARAMS,
        cost_estimate=cost(piece, 40),
    )(ready, half, table, own, other, in_hbm(old))


def last_step(shape, mine, half, table, low, high, enters, olds, out):
    slices, planes, width = shape
    pieces = pieces_of(width)
    operands = [half, table, low, high, enters, *map(in_vmem, olds)] + ([] if out is None else [in_hbm(out)])
    return pl.pallas_call(
        functools.partial(last_kernel, mine, pieces),
        in_specs=[SMEM] + [VMEM] * (4 + len(olds)) + ([] if out is None else [HBM]),
        out_shape=hbm(shape),
        out_specs=HBM,
        input_output_aliases={} if out is None else {len(operands) - 1: 0},
        scratch_shapes=[
            pltpu.VMEM((slices, planes // 2, width), jnp.float32),
            pltpu.SemaphoreType.DMA((sum(len(chunks_of(*piece)) for piece in pieces),)),
        ],
        compiler_params=PARAMS,
        cost_estimate=cost((slices, planes // 2, width), 6),
    )(*operands)


class Loop:
    def __init__(self):
        self.devices = lax.axis_size("tm")
        self.me = lax.axis_index("tm")
        self.levels = self.devices.bit_length() - 1
        assert self.devices == 1 << self.levels and self.levels > 3

    def swap(self, array, offset):
        return lax.ppermute(array, "tm", [(i, i ^ offset) for i in range(self.devices)])

    def rho(self, level):
        return self.arcs[level : level + 1]

    def is_left(self, level):
        return (self.me >> level) & 1 == 0

    def merge(self, mine, theirs, level):
        left, rho = self.is_left(level), self.rho(level)
        ours, others = jnp.where(left, rho, 1.0), jnp.where(left, 1.0, rho)
        return jnp.stack([ours * mine[0] + others * theirs[0], others * mine[1] + ours * theirs[1]])

    def down(self, mine, theirs, both, level):
        left, rho = self.is_left(level), self.rho(level)
        before = jnp.where(left, both[0], theirs[0] + rho * both[0])
        after = jnp.where(left, theirs[1] + rho * both[1], both[1])
        return jnp.stack([before, after])

    def down_other(self, mine, theirs, both, level):
        left, rho = self.is_left(level), self.rho(level)
        before = jnp.where(left, mine[0] + rho * both[0], both[0])
        after = jnp.where(left, both[1], mine[1] + rho * both[1])
        return jnp.stack([before, after])

    def solve(self, ends, arcs, works):
        self.arcs = arcs
        half = ends.shape[1] // 2
        bit = self.me & 1
        mine0 = lax.dynamic_slice_in_dim(ends, bit * half, half, 1)
        theirs0 = self.swap(lax.dynamic_slice_in_dim(ends, (1 - bit) * half, half, 1), 1)
        chip = self.merge(mine0, theirs0, 0)

        group = (self.me >> 1) & 3
        quarter = half // 4

        def part(k):
            return lax.dynamic_slice_in_dim(chip, (group ^ k) * quarter, quarter, 1)

        a0 = part(0)
        received = [self.swap(part(k), 2 * k) for k in (1, 2, 3)]
        state = works[0](chip)
        (a1, a2, a3), state = lax.optimization_barrier((received, state))
        near, far = self.merge(a0, a1, 1), self.merge(a2, a3, 1)
        arc = self.merge(near, far, 2)
        stack = []
        for level in range(3, self.levels):
            theirs = self.swap(arc, 1 << level)
            if level == 3:
                state = works[1](arc, state)
                theirs, state = lax.optimization_barrier((theirs, state))
            stack.append((arc, theirs, level))
            arc = self.merge(arc, theirs, level)
        enters = arc * self.rho(self.levels)
        for mine, theirs, level in reversed(stack):
            enters = self.down(mine, theirs, enters, level)
        enters_near = self.down(near, far, enters, 2)
        enters_far = self.down_other(near, far, enters, 2)
        p0 = self.down(a0, a1, enters_near, 1)
        p1 = self.down_other(a0, a1, enters_near, 1)
        p2 = self.down(a2, a3, enters_far, 1)
        p3 = self.down_other(a2, a3, enters_far, 1)
        received = [self.swap(p, 2 * k) for k, p in ((1, p1), (2, p2), (3, p3))]
        state = works[2](enters, state)
        received, state = lax.optimization_barrier((received, state))
        back = jnp.stack([p0] + received)
        chip_enters = jnp.concatenate(
            [lax.dynamic_index_in_dim(back, group ^ k, 0, keepdims=False) for k in range(4)], axis=1
        )
        own = self.down(mine0, theirs0, chip_enters, 0)
        other = self.swap(self.down_other(mine0, theirs0, chip_enters, 0), 1)
        return own, other, state


class Planes:
    def __init__(self, planes):
        self.planes = planes
        self.devices = lax.axis_size("space")
        self.me = lax.axis_index("space")
        self.rounds = [p for p in (0, 1) if p + 1 < self.devices]

    def row(self, parity):
        return jnp.where(self.me % 2 == parity, self.planes - 1, 0)

    def exchange(self, plane):
        low = high = 0.0
        for parity in self.rounds:
            row = self.row(parity)
            pairs = range(parity, self.devices - 1, 2)
            got = lax.ppermute(plane(row), "space", [(i, i + 1) for i in pairs] + [(i + 1, i) for i in pairs])
            low = low + jnp.where(row == 0, got, 0.0)
            high = high + jnp.where(row == 0, 0.0, got)
        return low, high


def on_device(field, step, mass):
    shape = _, planes, width = field.shape
    loop = Loop()
    sides = Planes(planes)
    half = (loop.me & 1).astype(jnp.int32).reshape(1)

    pieces = pieces_of(width)

    def sums_of(plane):
        return jnp.sum(weights[2:] * plane[None], axis=1)

    def with_edges(ends, first, last):
        row = lax.broadcasted_iota(jnp.int32, (1, planes, 1), 1)
        for place, sums in ((0, first), (planes - 1, last)):
            ends = ends - jnp.where(row == place, sums[:, None, :], 0.0)
        return ends

    low, high = sides.exchange(lambda row: lax.dynamic_index_in_dim(field, row, 1, keepdims=False))
    ends, table, weights, arcs, green = first_sums(step, mass, field, loop.levels)

    def first_work(tiles, ready, state=(None, ())):
        psi, edge = first_relax(tiles, ready, table, low, high, field, state[0])
        return psi, (*state[1], edge)

    works = [functools.partial(first_work, tiles) for tiles in pieces]
    own, other, (psi, edges) = loop.solve(with_edges(ends, sums_of(low), sums_of(high)), arcs, works)

    edges = jnp.concatenate(edges, axis=2)
    mine = half[0] == 0
    fluxes = jnp.where(mine, own[:, 0], other[:, 0]), jnp.where(mine, other[:, -1], own[:, -1])
    first, last = (edge - weights[0] * flux[0] - weights[1] * flux[1] for edge, flux in zip(edges, fluxes))
    halo = lambda row: jnp.where(row == 0, first, last)
    sums = sides.exchange(lambda row: sums_of(halo(row)))
    ends = with_edges(next_sums(half, table, own, other, psi), *sums)
    ends, first, last = lax.optimization_barrier((ends, first, last))
    low, high = sides.exchange(halo)

    def next_work(tiles, ready, state=(), own=own, other=other):
        return *state, next_relax(tiles, ready, half, own, other, table, psi)

    works = [functools.partial(next_work, tiles) for tiles in pieces]
    own, other, olds = loop.solve(ends, arcs, works)
    low, high = (jnp.dot(green[:, : field.shape[0]], plane, precision=lax.Precision.HIGHEST) for plane in (low, high))
    out = last_step(shape, True, half, table, low, high, own, olds, None)
    return last_step(shape, False, half, table, low, high, other, olds, out)


def solution(mesh):
    return jax.shard_map(
        on_device,
        mesh=mesh,
        in_specs=(P("tm", "space", None), P(), P()),
        out_specs=P("tm", "space", None),
        check_vma=False,
    )
```
